32 devices in a mesh: patch: 8 (over z, core), expert: 4 (over y, x).
Axes of the slice: x: 2, y: 2, z: 4, core: 2. Of those that a mesh axis runs over, the one named last changes fastest.
Arguments:
- latent: bfloat16 [4, 1024, 1152], P('expert', 'patch'), may hold values from -6 to 6
- stale_kv: bfloat16 [4, 1024, 1152], P('expert', 'patch'), may hold values from -300 to 300
- modulation: float32 [1, 6, 1152], replicated, may hold values from -3 to 3
- routes: int32 [1, 4, 1024, 2], P(None, 'expert', 'patch'), may hold values from 0 to 3, all different within a row; in each aligned block of 128 rows (0 to 127, 128 to 255, ..., all dimensions but the last counted through in order) at most 80 rows name the same one
- w_qkv: bfloat16 [1152, 1728], replicated, may hold values from -0.1875 to 0.1875
- w_attn_out: bfloat16 [576, 1152], replicated, may hold values from -0.25 to 0.25
- router: bfloat16 [1152, 4], replicated, may hold values from -0.1875 to 0.1875
- w_in: bfloat16 [4, 1152, 2304], P('expert', 'patch'), may hold values from -0.1875 to 0.1875
- w_out: bfloat16 [4, 2304, 1152], P('expert', 'patch'), may hold values from -0.125 to 0.125
Outputs:
- latent_out: bfloat16 [4, 1024, 1152], P('expert', 'patch')
- fresh_kv: bfloat16 [4, 1024, 1152], P('expert', 'patch')
The draws below stay inside these ranges and needn't reach their ends.
Inputs may be any that keep to these rules, and one draw needn't show every extreme that they name: A patch's two routes name different experts. In each step, clip and aligned block of 128 patches (the patches of one device) no expert is named by more than 80 routes, and in every draw some block names some expert exactly 80 times.
All inputs are finite; a program needn't handle non-finite values.
Results may differ from the reference program's by a relative error of at most 0.009.
Values may be sent and summed in bfloat16 or wider, within the bound.
A program may use at most 128 MiB of HBM per device.

```python
import math
import jax
import jax.numpy as jnp
import numpy as np
from jax import lax

D = 1152
HEADS = 8
HEAD_DIM = 72
FFW = 2304
STEPS = 1
TOK_DEV = 128
EXPERTS = 4
SEQS = 4
SEQ = 1024
CAP = 80
N_PATCH = 8


def draw_stale_kv(key, part):
    key = jax.random.fold_in(key, 7)
    first = jax.random.fold_in(key, 0)
    width = 2 * HEADS * HEAD_DIM
    base = jnp.clip(jax.random.normal(first, (SEQS, SEQ, width), jnp.float32), -5.0, 5.0)
    return base.astype(jnp.bfloat16)


def block_scale(rng, shape, cuts, low, top_value):
    gain, own = 1.0, jax.random.fold_in(rng, 6)
    for axis_at, shards_of in cuts:
        heights = jnp.exp(jax.random.uniform(jax.random.fold_in(own, axis_at), (shards_of,), jnp.float32, low / len(cuts), top_value / len(cuts)))
        gain = gain * jnp.repeat(heights, shape[axis_at] // shards_of).reshape([-1 if axis == axis_at else 1 for axis in range(len(shape))])
    return gain


def routed_block(rng, own, number, rows, count, top, bound, skew):
    ranking = jax.random.permutation(rng, count)
    packed, ordinary = portions_of(count, rows * top, bound, skew, True), portions_of(count, rows * top, bound, skew, False)
    places = jnp.arange(count)

    def named(sizes, rotation):
        used = int((sizes > 0).sum())
        fixed = max(1, used // 4)
        moved = fixed + (places - fixed + rotation * (used - fixed)) % max(1, count - fixed)
        return jnp.zeros((count,), jnp.int32).at[ranking[jnp.where(places < fixed, places, moved)]].set(jnp.asarray(sizes, jnp.int32))

    sizes = jnp.where(number % 4 == 0, named(packed, number // 4), named(ordinary, number - number // 4 - 1))
    mixed = jax.random.permutation(jax.random.fold_in(own, 3), count)
    donor, receiver = mixed[0:count // 2 * 2:2], mixed[1:count // 2 * 2:2]
    margin = jnp.minimum(sizes[donor] - 1, bound - sizes[receiver]) // 2
    margin = jnp.where((donor == ranking[0]) | (receiver == ranking[0]) | (sizes[receiver] == 0), 0, jnp.maximum(margin, 0))
    moved = jax.random.randint(jax.random.fold_in(own, 4), (count // 2,), 0, 1 << 20) % (margin + 1)
    sizes = sizes.at[donor].add(-moved).at[receiver].add(moved)
    items = jnp.searchsorted(jnp.cumsum(sizes), jnp.arange(rows * top), side="right").astype(jnp.int32)
    grid = items.reshape(top, rows).T
    grid = grid[jax.random.permutation(jax.random.fold_in(own, 1), rows)]
    rotation = jax.random.randint(jax.random.fold_in(own, 2), (rows, 1), 0, top)
    return jnp.take_along_axis(grid, (jnp.arange(top)[None, :] + rotation) % top, axis=1)


def portions_of(number_of, total, most, skew, full):
    weights = [(1 << 20) // math.isqrt(standing ** skew) + 1 for standing in range(1, number_of + 1)]
    largest = most if full else min(most, max(-(-total // number_of), total * weights[0] // sum(weights)))
    least = 1 if total - largest >= number_of - 1 else 0
    given, rest = [largest] + [least] * (number_of - 1), total - largest - least * (number_of - 1)
    while rest > 0:
        movable = [i for i in range(1, number_of) if given[i] < largest] or [i for i in range(1, number_of) if given[i] < most]
        whole, budget = sum([weights[i] for i in movable]), rest
        for i in movable:
            extra = min(most - given[i], max(1, budget * weights[i] // whole), rest)
            given[i] = given[i] + extra
            rest = rest - extra
    return np.array(given)


def normal_values(rng, dims, deviation, reach, pieces=(), kind=jnp.bfloat16):
    loudness = block_scale(rng, dims, pieces, -0.22, 0.18) if pieces else 1.0
    drawn = jax.random.normal(rng, dims, jnp.float32) * deviation * loudness
    return jnp.minimum(jnp.maximum(drawn, -reach), reach).astype(kind)


def setup_inputs(seed: int = 0) -> dict:
    seeds = jax.random.split(jax.random.key(seed), 10)
    latent = normal_values(seeds[0], (SEQS, SEQ, D), 1.0, 6.0, ((0, 4), (1, 8)))
    stale_kv = draw_stale_kv(jax.random.fold_in(seeds[9], 71), 0)
    modulation = normal_values(seeds[2], (STEPS, 6, D), 0.5, 3.0, (), jnp.float32)
    routes_keys = jax.random.split(jax.random.fold_in(seeds[3], 1), STEPS * SEQS * SEQ // TOK_DEV)
    routes_turns = jax.random.permutation(jax.random.fold_in(seeds[3], 3), STEPS * SEQS * SEQ // TOK_DEV)
    routes = jax.vmap(lambda own, number: routed_block(jax.random.fold_in(seeds[3], 2), own, number, TOK_DEV, EXPERTS, 2, CAP, 2))(routes_keys, routes_turns).reshape((STEPS, SEQS, SEQ, 2))
    w_qkv = normal_values(seeds[4], (D, 3 * HEADS * HEAD_DIM), D ** -0.5, 0.1875)
    w_attn_out = normal_values(seeds[5], (HEADS * HEAD_DIM, D), (HEADS * HEAD_DIM) ** -0.5, 0.25)
    router = normal_values(seeds[6], (D, EXPERTS), D ** -0.5, 0.1875)
    w_in = normal_values(seeds[7], (EXPERTS, D, FFW), D ** -0.5, 0.1875, ((0, 4), (1, 8)))
    w_out = normal_values(seeds[8], (EXPERTS, FFW, D), FFW ** -0.5, 0.125, ((0, 4), (1, 8)))
    return {"latent": latent, "stale_kv": stale_kv, "modulation": modulation, "routes": routes, "w_qkv": w_qkv, "w_attn_out": w_attn_out, "router": router, "w_in": w_in, "w_out": w_out}


EPSILON = 1e-06

def normalize(values, shift, scale):
    widened = values.astype(jnp.float32)
    center = lax.optimization_barrier(jnp.mean(widened, axis=-1, keepdims=True))
    spread = lax.optimization_barrier(jnp.mean(jnp.square(widened - center), axis=-1, keepdims=True))
    return ((widened - center) * lax.rsqrt(spread + EPSILON) * (1.0 + scale) + shift).astype(jnp.bfloat16)

def attend_sequence(query, current, previous):
    attn_width = HEADS * HEAD_DIM
    owner = jnp.arange(SEQ, dtype=jnp.int32) // TOK_DEV

    def one_block(block):
        query_rows = lax.dynamic_slice_in_dim(query, (block * TOK_DEV).astype(jnp.int32), TOK_DEV, 0)
        mixed = jnp.where((owner == block)[:, None], current, previous)
        keys = mixed[:, :attn_width].reshape(SEQ, HEADS, HEAD_DIM).astype(jnp.float32)
        values = mixed[:, attn_width:].reshape(SEQ, HEADS, HEAD_DIM).astype(jnp.float32)
        heads = query_rows.reshape(TOK_DEV, HEADS, HEAD_DIM).astype(jnp.float32)
        scores = jnp.einsum('qhd,khd->hqk', heads, keys) * HEAD_DIM ** (-0.5)
        highest = lax.optimization_barrier(jnp.max(scores, axis=-1, keepdims=True))
        weights = jnp.exp(scores - highest)
        totals = lax.optimization_barrier(jnp.sum(weights, axis=-1))
        rounded = lax.optimization_barrier(weights.astype(jnp.bfloat16)).astype(jnp.float32)
        summed = jnp.einsum('hqk,khd->qhd', rounded, values)
        result = summed / jnp.transpose(totals)[:, :, None]
        return result.reshape(TOK_DEV, attn_width).astype(jnp.bfloat16)
    return lax.map(one_block, jnp.arange(N_PATCH, dtype=jnp.int32)).reshape(SEQ, attn_width)

def expert_mix(normed, route_ids, router, w_in, w_out):
    block_count = SEQS * N_PATCH
    blocks = normed.reshape(block_count, TOK_DEV, D)
    chosen = route_ids.reshape(block_count, TOK_DEV, 2)
    logits = jnp.dot(normed.reshape(-1, D), router, preferred_element_type=jnp.float32).reshape(block_count, TOK_DEV, EXPERTS)
    onehot = chosen[..., None] == jnp.arange(EXPERTS, dtype=jnp.int32)
    gates = jax.nn.sigmoid(lax.optimization_barrier(jnp.sum(jnp.where(onehot, logits[:, :, None, :], 0.0), axis=-1)))
    flat = onehot.reshape(block_count, 2 * TOK_DEV, EXPERTS).astype(jnp.int32)
    slots = lax.optimization_barrier(jnp.sum((jnp.cumsum(flat, axis=1).astype(jnp.int32) - flat) * flat, axis=-1)).astype(jnp.int32)
    expert_ids = chosen.reshape(block_count, 2 * TOK_DEV)
    block_ids = jnp.broadcast_to(jnp.arange(block_count, dtype=jnp.int32)[:, None], expert_ids.shape)
    token_ids = jnp.broadcast_to((jnp.arange(2 * TOK_DEV, dtype=jnp.int32) // 2)[None, :], expert_ids.shape)
    table = jnp.full((EXPERTS, block_count, CAP), TOK_DEV, jnp.int32).at[expert_ids, block_ids, slots].set(token_ids)
    padded = jnp.concatenate([blocks, jnp.zeros((block_count, 1, D), blocks.dtype)], axis=1)
    row_index = jnp.arange(block_count, dtype=jnp.int32)[:, None]

    def run_expert(items):
        entries, weight_in, weight_out = items
        rows = padded[row_index, entries].reshape(block_count * CAP, D)
        hidden = jax.nn.gelu(jnp.dot(rows, weight_in, preferred_element_type=jnp.float32), approximate=True).astype(jnp.bfloat16)
        produced = jnp.dot(hidden, weight_out, preferred_element_type=jnp.float32).astype(jnp.bfloat16)
        return produced.reshape(block_count, CAP, D)
    results = lax.map(run_expert, (table, w_in, w_out))
    picked = results[expert_ids, block_ids, slots].astype(jnp.float32).reshape(block_count, TOK_DEV, 2, D)
    return lax.optimization_barrier(jnp.sum(picked * gates[..., None], axis=2)).reshape(SEQS, SEQ, D)

def reference(latent, stale_kv, modulation, routes, w_qkv, w_attn_out, router, w_in, w_out):
    attn_width = HEADS * HEAD_DIM
    state = latent
    previous = stale_kv
    for step_index in range(STEPS):
        shifts = modulation[step_index]
        normed = normalize(state, shifts[0], shifts[1])
        merged = jnp.dot(normed.reshape(-1, D), w_qkv, preferred_element_type=jnp.float32).astype(jnp.bfloat16)
        merged = merged.reshape(SEQS, SEQ, 3 * attn_width)
        query = merged[..., :attn_width]
        current = merged[..., attn_width:]
        attended = lax.map(lambda items: attend_sequence(items[0], items[1], items[2]), (query, current, previous))
        projected = jnp.dot(attended.reshape(-1, attn_width), w_attn_out, preferred_element_type=jnp.float32).reshape(SEQS, SEQ, D)
        middle = (state.astype(jnp.float32) + shifts[2] * projected).astype(jnp.bfloat16)
        normed_two = normalize(middle, shifts[3], shifts[4])
        mixture = expert_mix(normed_two, routes[step_index], router, w_in, w_out)
        state = (middle.astype(jnp.float32) + shifts[5] * mixture).astype(jnp.bfloat16)
        previous = current
    return (state, previous)
```

```python
import functools

import jax
import jax.numpy as jnp
from jax import lax
from jax.experimental import pallas as pl
from jax.experimental.pallas import tpu as pltpu
from jax.sharding import PartitionSpec as P

HEADS = 8


EPSILON = 1e-06


def normalize(values, shift, scale):
    widened = values.astype(jnp.float32)
    center = jnp.mean(widened, axis=-1, keepdims=True)
    spread = jnp.mean(jnp.square(widened - center), axis=-1, keepdims=True)
    return ((widened - center) * lax.rsqrt(spread + EPSILON) * (1.0 + scale) + shift).astype(
        jnp.bfloat16
    )


def attend_keys(query, current, previous, own_start, head_count):
    token_count, attn_width = query.shape
    head_size = attn_width // head_count
    factor = head_size ** (-0.5)
    query_heads = query.reshape(token_count, head_count, head_size)

    def scores_of(kv_rows):
        keys = kv_rows[:, :attn_width].reshape(kv_rows.shape[0], head_count, head_size)
        return (
            jnp.einsum("qhd,khd->hqk", query_heads, keys, preferred_element_type=jnp.float32)
            * factor
        )

    def values_of(kv_rows):
        return kv_rows[:, attn_width:].reshape(kv_rows.shape[0], head_count, head_size)

    own_scores = scores_of(current)
    highest = jnp.max(own_scores, axis=-1)
    weights = jnp.exp(own_scores - highest[..., None])
    totals = jnp.sum(weights, axis=-1)
    summed = jnp.einsum(
        "hqk,khd->hqd",
        weights.astype(jnp.bfloat16),
        values_of(current),
        preferred_element_type=jnp.float32,
    )
    best = highest
    mass = totals
    accum = summed
    rows = lax.all_gather(previous[None], "patch", axis=1, tiled=True)[0]
    positions = jnp.arange(rows.shape[0], dtype=jnp.int32)
    foreign = (positions < own_start) | (positions >= own_start + token_count)
    scores = jnp.where(foreign[None, None, :], scores_of(rows), -1e30)
    renewed = jnp.maximum(best, jnp.max(scores, axis=-1))
    decay = jnp.exp(best - renewed)
    fresh = jnp.exp(scores - renewed[..., None])
    mass = mass * decay + jnp.sum(fresh, axis=-1)
    added = jnp.einsum(
        "hqk,khd->hqd",
        fresh.astype(jnp.bfloat16),
        values_of(rows),
        preferred_element_type=jnp.float32,
    )
    best, mass, accum = (renewed, mass, accum * decay[..., None] + added)
    result = accum / mass[..., None]
    return jnp.transpose(result, (1, 0, 2)).reshape(token_count, attn_width).astype(jnp.bfloat16)


def expert_block(normed, chosen, router, weight_in, weight_out, capacity):
    token_count, width = normed.shape
    expert_count = router.shape[1]
    logits = jnp.dot(normed, router, preferred_element_type=jnp.float32)
    onehot = chosen[..., None] == jnp.arange(expert_count, dtype=jnp.int32)
    gates = jax.nn.sigmoid(jnp.sum(jnp.where(onehot, logits[:, None, :], 0.0), axis=-1))
    flat = onehot.reshape(2 * token_count, expert_count).astype(jnp.int32)
    slots = jnp.sum((jnp.cumsum(flat, axis=0) - flat) * flat, axis=-1)
    targets = chosen.reshape(-1) * capacity + slots
    columns = jnp.arange(expert_count * capacity, dtype=jnp.int32)
    placement = jnp.sum(
        (targets.reshape(token_count, 2)[:, :, None] == columns[None, None, :]).astype(
            jnp.bfloat16
        ),
        axis=1,
    )
    outgoing = jnp.einsum(
        "ts,td->sd", placement, normed, preferred_element_type=jnp.float32
    ).astype(jnp.bfloat16)
    outgoing = outgoing.reshape(expert_count, capacity, width)
    arrived = lax.all_to_all(outgoing, "expert", split_axis=0, concat_axis=0, tiled=True)
    flat_rows = arrived.reshape(expert_count * capacity, width)
    hidden = jax.nn.gelu(
        jnp.dot(flat_rows, weight_in, preferred_element_type=jnp.float32), approximate=True
    ).astype(jnp.bfloat16)
    produced = jnp.dot(hidden, weight_out, preferred_element_type=jnp.float32).astype(jnp.bfloat16)
    returned = lax.all_to_all(
        produced.reshape(expert_count, capacity, width),
        "expert",
        split_axis=0,
        concat_axis=0,
        tiled=True,
    )
    picked = (
        returned.reshape(expert_count * capacity, width)[targets]
        .astype(jnp.float32)
        .reshape(token_count, 2, width)
    )
    return jnp.sum(picked * gates[..., None], axis=1)


def on_device(latent, stale_kv, modulation, routes, w_qkv, w_attn_out, router, w_in, w_out):
    token_count = latent.shape[1]
    attn_width = w_attn_out.shape[0]
    expert_groups = lax.axis_size("expert")
    capacity = min(token_count, 5 * token_count // (2 * expert_groups))
    full_in, full_out = (
        lax.all_gather(w_in, "patch", axis=1, tiled=True),
        lax.all_gather(w_out, "patch", axis=1, tiled=True),
    )
    full_in = full_in[0]
    full_out = full_out[0]
    own_start = lax.axis_index("patch") * token_count
    state = latent[0]
    previous = stale_kv[0]
    shifts = modulation[0]
    normed = normalize(state, shifts[0], shifts[1])
    merged = jnp.dot(normed, w_qkv, preferred_element_type=jnp.float32).astype(jnp.bfloat16)
    query = merged[:, :attn_width]
    current = merged[:, attn_width:]
    attended = attend_keys(query, current, previous, own_start, HEADS)
    projected = jnp.dot(attended, w_attn_out, preferred_element_type=jnp.float32)
    middle = (state.astype(jnp.float32) + shifts[2] * projected).astype(jnp.bfloat16)
    normed_two = normalize(middle, shifts[3], shifts[4])
    mixture = expert_block(normed_two, routes[0, 0], router, full_in, full_out, capacity)
    state = (middle.astype(jnp.float32) + shifts[5] * mixture).astype(jnp.bfloat16)
    return (state[None], current[None])


MESH = pl.DeviceIdType.MESH
TO_PARTNER, TO_MIDDLE, TO_CORE = 0, 1, 2


def block_kernel(
    capacity,
    latent_ref, stale_ref, mod_ref, routes_ref, wqkv_hbm, wattn_hbm, router_ref, win_hbm, wout_hbm,
    out_ref, fresh_ref,
    kv, wqkv, wattn, win, wout, outgoing, rows, hidden, partial, produced, returned, attended,
    load_sem, send_sem, recv_sem, go_send, go_recv, back_send, back_recv,
):
    patch, expert = lax.axis_index("patch"), lax.axis_index("expert")
    z, core = patch // 2, patch % 2
    other = z * 2 + (1 - core)
    partner = (z + 1 - 2 * (z % 2)) * 2 + core
    across = (3 - z) * 2 + core
    far = (3 - partner // 2) * 2 + core
    middle_plane = (z == 1) | (z == 2)
    end_plane = (z == 0) | (z == 3)
    tokens, width = latent_ref.shape
    attn = wattn_hbm.shape[0]
    head_size = attn // HEADS
    experts = router_ref.shape[1]
    ffw = win_hbm.shape[1]

    buffers = (kv, win, wout)
    owned = (stale_ref, win_hbm, wout_hbm)

    def slot(which, index):
        count = owned[which].shape[0]
        return buffers[which].at[pl.ds(pl.multiple_of(index * count, 16), count)]

    def transfer(which, kind, index, own=False):
        target = (partner, across, other)[kind]
        return pltpu.make_async_remote_copy(
            src_ref=owned[which] if own else slot(which, index),
            dst_ref=slot(which, index),
            send_sem=send_sem.at[which, kind, index],
            recv_sem=recv_sem.at[which, index],
            device_id=(target, expert),
            device_id_type=MESH,
        )

    def arrived(which, index):
        transfer(which, TO_CORE, index).wait_recv()

    load_qkv = pltpu.make_async_copy(wqkv_hbm, wqkv, load_sem.at[0])
    load_attn = pltpu.make_async_copy(
        wattn_hbm, wattn.at[pl.ds(wattn.shape[0] - attn, attn)], load_sem.at[1]
    )
    load_qkv.start()
    load_attn.start()
    own_in = pltpu.make_async_copy(win_hbm, slot(1, patch), load_sem.at[2])
    own_out = pltpu.make_async_copy(wout_hbm, slot(2, patch), load_sem.at[3])

    @pl.when(middle_plane)
    def _():
        own_in.start()
        own_out.start()

    barrier = pltpu.get_barrier_semaphore()
    peers = [(other, expert), (partner, expert), (across, expert)]
    for step in range(1, experts):
        peers.append((patch, (expert + step) % experts))
        peers.append((partner, (expert + step) % experts))
    for peer in peers:
        pl.semaphore_signal(barrier, inc=1, device_id=peer, device_id_type=MESH)
    pl.semaphore_wait(barrier, len(peers))

    transfer(0, TO_PARTNER, patch, True).start()
    transfer(0, TO_CORE, patch, True).start()

    @pl.when(middle_plane)
    def _():
        transfer(0, TO_MIDDLE, patch, True).start()

    @pl.when(end_plane)
    def _():
        transfer(1, TO_PARTNER, patch, True).start()
        transfer(2, TO_PARTNER, patch, True).start()

    def row_of(index):
        return mod_ref[index : index + 1, :]

    normed = normalize(latent_ref[...], row_of(0), row_of(1))
    load_qkv.wait()
    merged = jnp.dot(normed, wqkv[...], preferred_element_type=jnp.float32)
    query = merged[:, : wattn.shape[0]].astype(jnp.bfloat16)
    current = merged[:, attn:].astype(jnp.bfloat16)
    fresh_ref[...] = current
    kv[pl.ds(pl.multiple_of(patch * tokens, 16), tokens), :] = current

    @pl.when(middle_plane)
    def _():
        arrived(0, partner)
        transfer(0, TO_MIDDLE, partner).start()
        transfer(0, TO_CORE, partner).start()
        arrived(0, across)
        transfer(0, TO_PARTNER, across).start()
        transfer(0, TO_CORE, across).start()
        transfer(1, TO_MIDDLE, patch, True).start()
        transfer(1, TO_CORE, patch, True).start()
        arrived(0, far)
        transfer(0, TO_PARTNER, far).start()
        transfer(0, TO_CORE, far).start()
        transfer(2, TO_MIDDLE, patch, True).start()
        transfer(2, TO_CORE, patch, True).start()

    @pl.when(end_plane)
    def _():
        for index in (partner, far, across):
            arrived(0, index)
            transfer(0, TO_CORE, index).start()

    for plane in range(4):
        arrived(0, plane * 2 + 1 - core)

    lead = wattn.shape[0] - attn
    base = attn - lead
    for head in range(HEADS):
        low, high = head * head_size, (head + 1) * head_size
        start, stop = low // 128 * 128, -(-high // 128) * 128
        column = lax.broadcasted_iota(jnp.int32, (tokens, stop - start), 1) + start
        chosen = jnp.where(
            (column >= low) & (column < high), query[:, start:stop].astype(jnp.float32), 0.0
        ).astype(jnp.bfloat16)
        scores = lax.dot_general(
            chosen, kv[:, start:stop], (((1,), (1,)), ((), ())), preferred_element_type=jnp.float32
        ) * head_size ** (-0.5)
        weights = jnp.exp(scores - jnp.max(scores, axis=-1, keepdims=True))
        total = jnp.sum(weights, axis=-1, keepdims=True)
        low, high = attn + low, attn + high
        start, stop = low // 128 * 128, -(-high // 128) * 128
        summed = (
            jnp.dot(
                weights.astype(jnp.bfloat16), kv[:, start:stop], preferred_element_type=jnp.float32
            )
            / total
        )
        column = lax.broadcasted_iota(jnp.int32, (tokens, stop - start), 1) + start
        mine = jnp.where((column >= low) & (column < high), summed, 0.0)
        first = start - base
        old = attended[:, first : first + stop - start]
        keep = (column < low) & (column >= attn)
        attended[:, first : first + stop - start] = jnp.where(keep, old, mine)

    @pl.when(middle_plane)
    def _():
        arrived(1, partner)
        transfer(1, TO_MIDDLE, partner).start()
        transfer(1, TO_CORE, partner).start()

    load_attn.wait()
    wattn[:lead, :] = jnp.zeros((lead, width), jnp.bfloat16)
    projected = jnp.dot(
        attended[...].astype(jnp.bfloat16), wattn[...], preferred_element_type=jnp.float32
    )
    middle = (latent_ref[...].astype(jnp.float32) + row_of(2) * projected).astype(jnp.bfloat16)
    out_ref[...] = middle
    normed_two = normalize(middle, row_of(3), row_of(4))
    logits = jnp.dot(normed_two, router_ref[...], preferred_element_type=jnp.float32)

    lane = lax.broadcasted_iota(jnp.int32, (tokens, 128), 1)
    line = lax.broadcasted_iota(jnp.int32, (tokens, tokens), 0)
    before = lax.broadcasted_iota(jnp.int32, (tokens, tokens), 1) < line
    named = ((routes_ref[:, 0:1] == lane) | (routes_ref[:, 1:2] == lane)).astype(jnp.float32)
    place = jnp.dot(
        before.astype(jnp.float32).astype(jnp.bfloat16),
        named.astype(jnp.bfloat16),
        preferred_element_type=jnp.float32,
    )
    place = jnp.where(named > 0.0, place, -1.0)
    place_t = place.T
    entry = lax.broadcasted_iota(jnp.int32, (capacity, tokens), 0).astype(jnp.float32)
    for index in range(experts):
        pick = (entry == place_t[index : index + 1, :]).astype(jnp.float32).astype(jnp.bfloat16)
        outgoing[index * capacity : (index + 1) * capacity, :] = jnp.dot(
            pick, normed_two, preferred_element_type=jnp.float32
        ).astype(jnp.bfloat16)

    def span(index):
        return pl.ds(pl.multiple_of(index * capacity, 16), capacity)

    def go(side, index):
        return pltpu.make_async_remote_copy(
            src_ref=outgoing.at[span(index)],
            dst_ref=rows.at[span(side * experts + expert)],
            send_sem=go_send.at[index],
            recv_sem=go_recv.at[side, expert],
            device_id=(partner if side else patch, index),
            device_id_type=MESH,
        )

    def back(side, index):
        return pltpu.make_async_remote_copy(
            src_ref=produced.at[span(side * experts + index)],
            dst_ref=returned.at[span(expert)],
            send_sem=back_send.at[side, index],
            recv_sem=back_recv.at[expert],
            device_id=(partner if side else patch, index),
            device_id_type=MESH,
        )

    def await_rows(side, source):
        pltpu.make_async_copy(
            outgoing.at[span(source)],
            rows.at[span(side * experts + source)],
            go_recv.at[side, source],
        ).wait()

    def await_back(source):
        pltpu.make_async_copy(
            outgoing.at[span(source)], returned.at[span(source)], back_recv.at[source]
        ).wait()

    @pl.when(end_plane)
    def _():
        for step in range(experts):
            go(1, (expert + step) % experts).start()

    @pl.when(middle_plane)
    def _():
        for step in range(1, experts):
            go(0, (expert + step) % experts).start()
        rows[span(expert), :] = outgoing[span(expert), :]
        arrived(2, partner)
        transfer(2, TO_MIDDLE, partner).start()
        transfer(2, TO_CORE, partner).start()
        for which in (1,):
            for index in (across, far):
                arrived(which, index)
                transfer(which, TO_CORE, index).start()
        own_in.wait()
        own_out.wait()
        for step in range(1, experts):
            await_rows(0, (expert + step) % experts)
        for step in range(experts):
            await_rows(1, (expert + step) % experts)
        for plane in range(4):
            arrived(1, plane * 2 + 1 - core)

        def first_layer(step, carry):
            columns = pl.ds(pl.multiple_of(step * 256, 256), 256)
            hidden[:, columns] = jax.nn.gelu(
                jnp.dot(rows[...], win[:, columns], preferred_element_type=jnp.float32),
                approximate=True,
            ).astype(jnp.bfloat16)
            return carry

        lax.fori_loop(0, ffw // 256, first_layer, 0)

        half = ffw // 2
        near_at = pl.multiple_of((z // 2) * half, 128)
        far_at = pl.multiple_of((1 - z // 2) * half, 128)
        arrived(2, other)
        arrived(2, partner + 1 - 2 * core)
        partial[...] = jnp.dot(
            hidden[:, pl.ds(near_at, half)],
            wout[pl.ds(near_at, half), :],
            preferred_element_type=jnp.float32,
        )
        for index in (across, far):
            arrived(2, index)
            transfer(2, TO_CORE, index).start()
        arrived(2, across + 1 - 2 * core)
        arrived(2, far + 1 - 2 * core)
        count = experts * capacity
        for side in (1, 0):
            block = slice(side * count, (side + 1) * count)
            produced[block, :] = (
                partial[block, :]
                + jnp.dot(
                    hidden[block, pl.ds(far_at, half)],
                    wout[pl.ds(far_at, half), :],
                    preferred_element_type=jnp.float32,
                )
            ).astype(jnp.bfloat16)
            for step in range(1 - side, experts):
                back(side, (expert + step) % experts).start()
        returned[span(expert), :] = produced[span(expert), :]
        for step in range(1, experts):
            await_back((expert + step) % experts)

    @pl.when(end_plane)
    def _():
        for step in range(experts):
            await_back((expert + step) % experts)

    mixture = jnp.zeros((tokens, width), jnp.float32)
    entry = lax.broadcasted_iota(jnp.int32, (tokens, capacity), 1).astype(jnp.float32)
    gates = jax.nn.sigmoid(logits)
    for index in range(experts):
        pick = (entry == place[:, index : index + 1]).astype(jnp.float32).astype(jnp.bfloat16)
        picked = jnp.dot(
            pick,
            returned[index * capacity : (index + 1) * capacity, :],
            preferred_element_type=jnp.float32,
        )
        mixture = mixture + picked * gates[:, index : index + 1]
    out_ref[...] = (out_ref[...].astype(jnp.float32) + row_of(5) * mixture).astype(jnp.bfloat16)

    transfer(0, TO_PARTNER, patch, True).wait_send()
    transfer(0, TO_CORE, patch, True).wait_send()
    for index in (partner, across, far):
        transfer(0, TO_CORE, index).wait_send()

    @pl.when(end_plane)
    def _():
        transfer(1, TO_PARTNER, patch, True).wait_send()
        transfer(2, TO_PARTNER, patch, True).wait_send()
        for step in range(experts):
            go(1, (expert + step) % experts).wait_send()

    @pl.when(middle_plane)
    def _():
        transfer(0, TO_MIDDLE, patch, True).wait_send()
        transfer(0, TO_MIDDLE, partner).wait_send()
        transfer(0, TO_PARTNER, across).wait_send()
        transfer(0, TO_PARTNER, far).wait_send()
        for which in (1, 2):
            transfer(which, TO_MIDDLE, patch, True).wait_send()
            transfer(which, TO_MIDDLE, partner).wait_send()
            transfer(which, TO_CORE, patch, True).wait_send()
            for index in (partner, across, far):
                transfer(which, TO_CORE, index).wait_send()
        for step in range(1, experts):
            go(0, (expert + step) % experts).wait_send()
            back(0, (expert + step) % experts).wait_send()
        for step in range(experts):
            back(1, (expert + step) % experts).wait_send()


def on_line(latent, stale_kv, modulation, routes, w_qkv, w_attn_out, router, w_in, w_out):
    tokens, width = latent.shape[1:]
    attn = w_attn_out.shape[0]
    experts, patches = lax.axis_size("expert"), lax.axis_size("patch")
    capacity = min(tokens, 5 * tokens // (2 * experts))
    ffw = w_in.shape[2]
    padded = -(-attn // 128) * 128
    slots = experts * capacity
    vmem, hbm = pl.BlockSpec(memory_space=pltpu.VMEM), pl.BlockSpec(memory_space=pl.ANY)
    narrow = jnp.bfloat16
    state, current = pl.pallas_call(
        functools.partial(block_kernel, capacity),
        out_shape=(
            jax.ShapeDtypeStruct((tokens, width), narrow),
            jax.ShapeDtypeStruct((tokens, 2 * attn), narrow),
        ),
        in_specs=[vmem, hbm, vmem, vmem, hbm, hbm, vmem, hbm, hbm],
        out_specs=(vmem, vmem),
        scratch_shapes=[
            pltpu.VMEM((patches * tokens, 2 * attn), narrow),
            pltpu.VMEM(w_qkv.shape, narrow),
            pltpu.VMEM((padded, width), narrow),
            pltpu.VMEM((width, ffw), narrow),
            pltpu.VMEM((ffw, width), narrow),
            pltpu.VMEM((slots, width), narrow),
            pltpu.VMEM((2 * slots, width), narrow),
            pltpu.VMEM((2 * slots, ffw), narrow),
            pltpu.VMEM((2 * slots, width), jnp.float32),
            pltpu.VMEM((2 * slots, width), narrow),
            pltpu.VMEM((slots, width), narrow),
            pltpu.VMEM((tokens, padded), jnp.float32),
            pltpu.SemaphoreType.DMA((4,)),
            pltpu.SemaphoreType.DMA((3, 3, patches)),
            pltpu.SemaphoreType.DMA((3, patches)),
            pltpu.SemaphoreType.DMA((experts,)),
            pltpu.SemaphoreType.DMA((2, experts)),
            pltpu.SemaphoreType.DMA((2, experts)),
            pltpu.SemaphoreType.DMA((experts,)),
        ],
        compiler_params=pltpu.CompilerParams(
            collective_id=0, has_side_effects=True, vmem_limit_bytes=56 * 1024 * 1024
        ),
    )(
        latent[0], stale_kv[0], modulation[0], routes[0, 0], w_qkv, w_attn_out, router,
        w_in[0], w_out[0],
    )
    return (state[None], current[None])


def solution(mesh):
    line_of_four = mesh.shape["patch"] == 8 and mesh.shape["expert"] == 4
    in_specs = (
        P("expert", "patch", None),
        P("expert", "patch", None),
        P(),
        P(None, "expert", "patch", None),
        P(),
        P(),
        P(),
        P("expert", "patch", None),
        P("expert", "patch", None),
    )
    out_specs = (P("expert", "patch", None), P("expert", "patch", None))
    return jax.shard_map(
        on_line if line_of_four else on_device, mesh=mesh, in_specs=in_specs, out_specs=out_specs, check_vma=False
    )
```

```python
import functools

import jax
import jax.numpy as jnp
from jax import lax
from jax.experimental import pallas as pl
from jax.experimental.pallas import tpu as pltpu
from jax.sharding import PartitionSpec as P

HEADS = 8


EPSILON = 1e-06


def normalize(values, shift, scale):
    widened = values.astype(jnp.float32)
    center = jnp.mean(widened, axis=-1, keepdims=True)
    spread = jnp.mean(jnp.square(widened - center), axis=-1, keepdims=True)
    return ((widened - center) * lax.rsqrt(spread + EPSILON) * (1.0 + scale) + shift).astype(
        jnp.bfloat16
    )


def attend_keys(query, current, previous, own_start, head_count):
    token_count, attn_width = query.shape
    head_size = attn_width // head_count
    factor = head_size ** (-0.5)
    query_heads = query.reshape(token_count, head_count, head_size)

    def scores_of(kv_rows):
        keys = kv_rows[:, :attn_width].reshape(kv_rows.shape[0], head_count, head_size)
        return (
            jnp.einsum("qhd,khd->hqk", query_heads, keys, preferred_element_type=jnp.float32)
            * factor
        )

    def values_of(kv_rows):
        return kv_rows[:, attn_width:].reshape(kv_rows.shape[0], head_count, head_size)

    own_scores = scores_of(current)
    highest = jnp.max(own_scores, axis=-1)
    weights = jnp.exp(own_scores - highest[..., None])
    totals = jnp.sum(weights, axis=-1)
    summed = jnp.einsum(
        "hqk,khd->hqd",
        weights.astype(jnp.bfloat16),
        values_of(current),
        preferred_element_type=jnp.float32,
    )
    best = highest
    mass = totals
    accum = summed
    rows = lax.all_gather(previous[None], "patch", axis=1, tiled=True)[0]
    positions = jnp.arange(rows.shape[0], dtype=jnp.int32)
    foreign = (positions < own_start) | (positions >= own_start + token_count)
    scores = jnp.where(foreign[None, None, :], scores_of(rows), -1e30)
    renewed = jnp.maximum(best, jnp.max(scores, axis=-1))
    decay = jnp.exp(best - renewed)
    fresh = jnp.exp(scores - renewed[..., None])
    mass = mass * decay + jnp.sum(fresh, axis=-1)
    added = jnp.einsum(
        "hqk,khd->hqd",
        fresh.astype(jnp.bfloat16),
        values_of(rows),
        preferred_element_type=jnp.float32,
    )
    best, mass, accum = (renewed, mass, accum * decay[..., None] + added)
    result = accum / mass[..., None]
    return jnp.transpose(result, (1, 0, 2)).reshape(token_count, attn_width).astype(jnp.bfloat16)


def expert_block(normed, chosen, router, weight_in, weight_out, capacity):
    token_count, width = normed.shape
    expert_count = router.shape[1]
    logits = jnp.dot(normed, router, preferred_element_type=jnp.float32)
    onehot = chosen[..., None] == jnp.arange(expert_count, dtype=jnp.int32)
    gates = jax.nn.sigmoid(jnp.sum(jnp.where(onehot, logits[:, None, :], 0.0), axis=-1))
    flat = onehot.reshape(2 * token_count, expert_count).astype(jnp.int32)
    slots = jnp.sum((jnp.cumsum(flat, axis=0) - flat) * flat, axis=-1)
    targets = chosen.reshape(-1) * capacity + slots
    columns = jnp.arange(expert_count * capacity, dtype=jnp.int32)
    placement = jnp.sum(
        (targets.reshape(token_count, 2)[:, :, None] == columns[None, None, :]).astype(
            jnp.bfloat16
        ),
        axis=1,
    )
    outgoing = jnp.einsum(
        "ts,td->sd", placement, normed, preferred_element_type=jnp.float32
    ).astype(jnp.bfloat16)
    outgoing = outgoing.reshape(expert_count, capacity, width)
    arrived = lax.all_to_all(outgoing, "expert", split_axis=0, concat_axis=0, tiled=True)
    flat_rows = arrived.reshape(expert_count * capacity, width)
    hidden = jax.nn.gelu(
        jnp.dot(flat_rows, weight_in, preferred_element_type=jnp.float32), approximate=True
    ).astype(jnp.bfloat16)
    produced = jnp.dot(hidden, weight_out, preferred_element_type=jnp.float32).astype(jnp.bfloat16)
    returned = lax.all_to_all(
        produced.reshape(expert_count, capacity, width),
        "expert",
        split_axis=0,
        concat_axis=0,
        tiled=True,
    )
    picked = (
        returned.reshape(expert_count * capacity, width)[targets]
        .astype(jnp.float32)
        .reshape(token_count, 2, width)
    )
    return jnp.sum(picked * gates[..., None], axis=1)


def on_device(latent, stale_kv, modulation, routes, w_qkv, w_attn_out, router, w_in, w_out):
    token_count = latent.shape[1]
    attn_width = w_attn_out.shape[0]
    expert_groups = lax.axis_size("expert")
    capacity = min(token_count, 5 * token_count // (2 * expert_groups))
    full_in, full_out = (
        lax.all_gather(w_in, "patch", axis=1, tiled=True),
        lax.all_gather(w_out, "patch", axis=1, tiled=True),
    )
    full_in = full_in[0]
    full_out = full_out[0]
    own_start = lax.axis_index("patch") * token_count
    state = latent[0]
    previous = stale_kv[0]
    shifts = modulation[0]
    normed = normalize(state, shifts[0], shifts[1])
    merged = jnp.dot(normed, w_qkv, preferred_element_type=jnp.float32).astype(jnp.bfloat16)
    query = merged[:, :attn_width]
    current = merged[:, attn_width:]
    attended = attend_keys(query, current, previous, own_start, HEADS)
    projected = jnp.dot(attended, w_attn_out, preferred_element_type=jnp.float32)
    middle = (state.astype(jnp.float32) + shifts[2] * projected).astype(jnp.bfloat16)
    normed_two = normalize(middle, shifts[3], shifts[4])
    mixture = expert_block(normed_two, routes[0, 0], router, full_in, full_out, capacity)
    state = (middle.astype(jnp.float32) + shifts[5] * mixture).astype(jnp.bfloat16)
    return (state[None], current[None])


MESH = pl.DeviceIdType.MESH
TO_PARTNER, TO_MIDDLE, TO_CORE = 0, 1, 2
CHUNKS = 3


def block_kernel(
    capacity,
    latent_ref, stale_ref, mod_ref, routes_ref, wqkv_hbm, wattn_hbm, router_ref, win_hbm, wout_hbm,
    out_ref, fresh_ref,
    kv, wqkv, wattn, win, wout, outgoing, rows, hidden, produced, returned, attended,
    load_sem, send_sem, recv_sem, go_send, go_recv, back_send, back_recv,
):
    patch, expert = lax.axis_index("patch"), lax.axis_index("expert")
    z, core = patch // 2, patch % 2
    other = z * 2 + (1 - core)
    partner = (z + 1 - 2 * (z % 2)) * 2 + core
    across = (3 - z) * 2 + core
    far = (3 - partner // 2) * 2 + core
    middle_plane = (z == 1) | (z == 2)
    end_plane = (z == 0) | (z == 3)
    tokens, width = latent_ref.shape
    attn = wattn_hbm.shape[0]
    head_size = attn // HEADS
    experts = router_ref.shape[0]
    ffw = win_hbm.shape[1]

    chunk = width // CHUNKS
    chunks = range(2, 2 + CHUNKS)
    buffers = [kv, win] + [wout.at[part] for part in range(CHUNKS)]
    owned = [stale_ref, win_hbm] + [
        wout_hbm.at[:, pl.ds(part * chunk, chunk)] for part in range(CHUNKS)
    ]

    def slot(which, index):
        count = owned[which].shape[0]
        return buffers[which].at[pl.ds(pl.multiple_of(index * count, 16), count)]

    def transfer(which, kind, index, own=False):
        target = (partner, across, other)[kind]
        return pltpu.make_async_remote_copy(
            src_ref=owned[which] if own else slot(which, index),
            dst_ref=slot(which, index),
            send_sem=send_sem.at[which, kind, index],
            recv_sem=recv_sem.at[which, index],
            device_id=(target, expert),
            device_id_type=MESH,
        )

    def arrived(which, index):
        transfer(which, TO_CORE, index).wait_recv()

    load_qkv = pltpu.make_async_copy(wqkv_hbm, wqkv, load_sem.at[0])
    load_attn = pltpu.make_async_copy(
        wattn_hbm, wattn.at[pl.ds(wattn.shape[0] - attn, attn)], load_sem.at[1]
    )
    load_qkv.start()
    load_attn.start()
    own_loads = [
        pltpu.make_async_copy(owned[which], slot(which, patch), load_sem.at[1 + which])
        for which in range(1, 2 + CHUNKS)
    ]

    @pl.when(middle_plane)
    def _():
        for load in own_loads:
            load.start()

    barrier = pltpu.get_barrier_semaphore()
    peers = [(other, expert), (partner, expert), (across, expert)]
    for step in range(1, experts):
        peers.append((patch, (expert + step) % experts))
        peers.append((partner, (expert + step) % experts))
    for peer in peers:
        pl.semaphore_signal(barrier, inc=1, device_id=peer, device_id_type=MESH)
    pl.semaphore_wait(barrier, len(peers))

    transfer(0, TO_PARTNER, patch, True).start()
    transfer(0, TO_CORE, patch, True).start()

    @pl.when(middle_plane)
    def _():
        transfer(0, TO_MIDDLE, patch, True).start()
        transfer(1, TO_MIDDLE, patch, True).start()

    @pl.when(end_plane)
    def _():
        for which in range(1, 2 + CHUNKS):
            transfer(which, TO_PARTNER, patch, True).start()

    def row_of(index):
        return mod_ref[index]

    def times_rows(left, right):
        return lax.dot_general(
            left, right, (((1,), (1,)), ((), ())), preferred_element_type=jnp.float32
        )

    normed = normalize(latent_ref[...], row_of(0), row_of(1))
    load_qkv.wait()
    query = times_rows(normed, wqkv[: wattn.shape[0], :]).astype(jnp.bfloat16)
    current = times_rows(normed, wqkv[attn:, :]).astype(jnp.bfloat16)
    fresh_ref[...] = current
    kv[pl.ds(pl.multiple_of(patch * tokens, 16), tokens), :] = current

    @pl.when(middle_plane)
    def _():
        arrived(0, partner)
        transfer(0, TO_MIDDLE, partner).start()
        transfer(0, TO_CORE, partner).start()
        arrived(0, across)
        transfer(0, TO_PARTNER, across).start()
        transfer(0, TO_CORE, across).start()
        arrived(0, far)
        transfer(0, TO_PARTNER, far).start()
        transfer(0, TO_CORE, far).start()
        transfer(2, TO_MIDDLE, patch, True).start()

    @pl.when(end_plane)
    def _():
        for index in (partner, far, across):
            arrived(0, index)
            transfer(0, TO_CORE, index).start()

    for plane in range(4):
        arrived(0, plane * 2 + 1 - core)

    lead = wattn.shape[0] - attn
    base = attn - lead
    for head in range(HEADS):
        low, high = head * head_size, (head + 1) * head_size
        start, stop = low // 128 * 128, -(-high // 128) * 128
        column = lax.broadcasted_iota(jnp.int32, (tokens, stop - start), 1) + start
        chosen = jnp.where(
            (column >= low) & (column < high), query[:, start:stop].astype(jnp.float32), 0.0
        ).astype(jnp.bfloat16)
        scores = times_rows(chosen, kv[:, start:stop]) * head_size ** (-0.5)
        weights = jnp.exp(scores - jnp.max(scores, axis=-1, keepdims=True))
        total = jnp.sum(weights, axis=-1, keepdims=True)
        low, high = attn + low, attn + high
        start, stop = low // 128 * 128, -(-high // 128) * 128
        summed = (
            jnp.dot(
                weights.astype(jnp.bfloat16), kv[:, start:stop], preferred_element_type=jnp.float32
            )
            / total
        )
        column = lax.broadcasted_iota(jnp.int32, (tokens, stop - start), 1) + start
        mine = jnp.where((column >= low) & (column < high), summed, 0.0)
        first = start - base
        old = attended[:, first : first + stop - start]
        keep = (column < low) & (column >= attn)
        attended[:, first : first + stop - start] = jnp.where(keep, old, mine)
        if head == HEADS // 2 - 1:

            @pl.when(middle_plane)
            def _():
                arrived(1, partner)
                transfer(1, TO_MIDDLE, partner).start()
                transfer(1, TO_CORE, partner).start()
                transfer(1, TO_CORE, patch, True).start()

    @pl.when(middle_plane)
    def _():
        arrived(2, partner)
        transfer(2, TO_MIDDLE, partner).start()
        transfer(3, TO_MIDDLE, patch, True).start()

    load_attn.wait()
    wattn[:lead, :] = jnp.zeros((lead, width), jnp.bfloat16)
    projected = jnp.dot(
        attended[...].astype(jnp.bfloat16), wattn[...], preferred_element_type=jnp.float32
    )
    middle = (latent_ref[...].astype(jnp.float32) + row_of(2) * projected).astype(jnp.bfloat16)
    out_ref[...] = middle
    normed_two = normalize(middle, row_of(3), row_of(4))
    logits = times_rows(normed_two, router_ref[...])

    line = lax.broadcasted_iota(jnp.int32, (tokens, tokens), 0)
    lane = lax.broadcasted_iota(jnp.int32, (tokens, tokens), 1)
    named = ((routes_ref[0:1, :] == line) | (routes_ref[1:2, :] == line)).astype(jnp.float32)
    place_t = jnp.dot(
        named.astype(jnp.bfloat16),
        (line < lane).astype(jnp.float32).astype(jnp.bfloat16),
        preferred_element_type=jnp.float32,
    )
    place_t = jnp.where(named > 0.0, place_t, -1.0)
    place = place_t.T
    entry = lax.broadcasted_iota(jnp.int32, (capacity, tokens), 0).astype(jnp.float32)
    for index in range(experts):
        pick = (entry == place_t[index : index + 1, :]).astype(jnp.float32).astype(jnp.bfloat16)
        outgoing[index * capacity : (index + 1) * capacity, :] = jnp.dot(
            pick, normed_two, preferred_element_type=jnp.float32
        ).astype(jnp.bfloat16)

    def span(index):
        return pl.ds(pl.multiple_of(index * capacity, 16), capacity)

    def go(side, index):
        return pltpu.make_async_remote_copy(
            src_ref=outgoing.at[span(index)],
            dst_ref=rows.at[span(side * experts + expert)],
            send_sem=go_send.at[index],
            recv_sem=go_recv.at[side, expert],
            device_id=(partner if side else patch, index),
            device_id_type=MESH,
        )

    def back(side, index, part):
        return pltpu.make_async_remote_copy(
            src_ref=produced.at[part, span(side * experts + index)],
            dst_ref=returned.at[part, span(expert)],
            send_sem=back_send.at[part, side, index],
            recv_sem=back_recv.at[part, expert],
            device_id=(partner if side else patch, index),
            device_id_type=MESH,
        )

    def await_rows(side, source):
        pltpu.make_async_copy(
            outgoing.at[span(source)],
            rows.at[span(side * experts + source)],
            go_recv.at[side, source],
        ).wait()

    def await_back(source, part):
        pltpu.make_async_copy(
            produced.at[part, span(source)],
            returned.at[part, span(source)],
            back_recv.at[part, source],
        ).wait()

    @pl.when(end_plane)
    def _():
        for step in range(experts):
            go(1, (expert + step) % experts).start()

    @pl.when(middle_plane)
    def _():
        for step in range(1, experts):
            go(0, (expert + step) % experts).start()
        rows[span(expert), :] = outgoing[span(expert), :]
        for which in chunks[1:]:
            arrived(which, partner)
            transfer(which, TO_MIDDLE, partner).start()
            if which + 1 in chunks:
                transfer(which + 1, TO_MIDDLE, patch, True).start()
        for index in (across, far):
            arrived(1, index)
            transfer(1, TO_CORE, index).start()
        for which in chunks:
            transfer(which, TO_CORE, patch, True).start()
            transfer(which, TO_CORE, partner).start()
        for load in own_loads:
            load.wait()
        for step in range(1, experts):
            await_rows(0, (expert + step) % experts)
        for step in range(experts):
            await_rows(1, (expert + step) % experts)
        for plane in range(4):
            arrived(1, plane * 2 + 1 - core)

        def first_layer(step, carry):
            columns = pl.ds(pl.multiple_of(step * 256, 256), 256)
            hidden[:, columns] = jax.nn.gelu(
                jnp.dot(rows[...], win[:, columns], preferred_element_type=jnp.float32),
                approximate=True,
            ).astype(jnp.bfloat16)
            return carry

        lax.fori_loop(0, ffw // 256, first_layer, 0)

        count = experts * capacity
        for part in range(CHUNKS):
            which = part + 2
            for index in (across, far):
                arrived(which, index)
                transfer(which, TO_CORE, index).start()
            for plane in range(4):
                arrived(which, plane * 2 + 1 - core)
            for side in (1, 0):
                block = slice(side * count, (side + 1) * count)
                produced[part, block, :] = jnp.dot(
                    hidden[block, :], wout[part], preferred_element_type=jnp.float32
                ).astype(jnp.bfloat16)
                for step in range(1 - side, experts):
                    back(side, (expert + step) % experts, part).start()
            returned[part, span(expert), :] = produced[part, span(expert), :]

    entry = lax.broadcasted_iota(jnp.int32, (tokens, capacity), 1).astype(jnp.float32)
    gates = jax.nn.sigmoid(logits)
    picks = [
        (entry == place[:, index : index + 1]).astype(jnp.float32).astype(jnp.bfloat16)
        for index in range(experts)
    ]
    for part in range(CHUNKS):
        for step in range(1, experts):
            await_back((expert + step) % experts, part)

        @pl.when(end_plane)
        def _():
            await_back(expert, part)

        columns = slice(part * chunk, (part + 1) * chunk)
        mixture = jnp.zeros((tokens, chunk), jnp.float32)
        for index in range(experts):
            picked = jnp.dot(
                picks[index],
                returned[part, index * capacity : (index + 1) * capacity, :],
                preferred_element_type=jnp.float32,
            )
            mixture = mixture + picked * gates[:, index : index + 1]
        out_ref[:, columns] = (
            out_ref[:, columns].astype(jnp.float32) + row_of(5)[:, columns] * mixture
        ).astype(jnp.bfloat16)

    transfer(0, TO_PARTNER, patch, True).wait_send()
    transfer(0, TO_CORE, patch, True).wait_send()
    for index in (partner, across, far):
        transfer(0, TO_CORE, index).wait_send()

    @pl.when(end_plane)
    def _():
        for which in range(1, 2 + CHUNKS):
            transfer(which, TO_PARTNER, patch, True).wait_send()
        for step in range(experts):
            go(1, (expert + step) % experts).wait_send()

    @pl.when(middle_plane)
    def _():
        transfer(0, TO_MIDDLE, patch, True).wait_send()
        transfer(0, TO_MIDDLE, partner).wait_send()
        transfer(0, TO_PARTNER, across).wait_send()
        transfer(0, TO_PARTNER, far).wait_send()
        for which in range(1, 2 + CHUNKS):
            transfer(which, TO_MIDDLE, patch, True).wait_send()
            transfer(which, TO_MIDDLE, partner).wait_send()
            transfer(which, TO_CORE, patch, True).wait_send()
            for index in (partner, across, far):
                transfer(which, TO_CORE, index).wait_send()
        for step in range(1, experts):
            go(0, (expert + step) % experts).wait_send()
        for part in range(CHUNKS):
            for side in (1, 0):
                for step in range(1 - side, experts):
                    back(side, (expert + step) % experts, part).wait_send()


def on_line(latent, stale_kv, modulation, routes, w_qkv, w_attn_out, router, w_in, w_out):
    tokens, width = latent.shape[1:]
    attn = w_attn_out.shape[0]
    experts, patches = lax.axis_size("expert"), lax.axis_size("patch")
    capacity = min(tokens, 5 * tokens // (2 * experts))
    ffw = w_in.shape[2]
    padded = -(-attn // 128) * 128
    slots = experts * capacity
    vmem, hbm = pl.BlockSpec(memory_space=pltpu.VMEM), pl.BlockSpec(memory_space=pl.ANY)
    narrow = jnp.bfloat16
    state, current = pl.pallas_call(
        functools.partial(block_kernel, capacity),
        out_shape=(
            jax.ShapeDtypeStruct((tokens, width), narrow),
            jax.ShapeDtypeStruct((tokens, 2 * attn), narrow),
        ),
        in_specs=[vmem, hbm, vmem, vmem, hbm, hbm, vmem, hbm, hbm],
        out_specs=(vmem, vmem),
        scratch_shapes=[
            pltpu.VMEM((patches * tokens, 2 * attn), narrow),
            pltpu.VMEM(w_qkv.shape[::-1], narrow),
            pltpu.VMEM((padded, width), narrow),
            pltpu.VMEM((width, ffw), narrow),
            pltpu.VMEM((CHUNKS, ffw, width // CHUNKS), narrow),
            pltpu.VMEM((slots, width), narrow),
            pltpu.VMEM((2 * slots, width), narrow),
            pltpu.VMEM((2 * slots, ffw), narrow),
            pltpu.VMEM((CHUNKS, 2 * slots, width // CHUNKS), narrow),
            pltpu.VMEM((CHUNKS, slots, width // CHUNKS), narrow),
            pltpu.VMEM((tokens, padded), jnp.float32),
            pltpu.SemaphoreType.DMA((3 + CHUNKS,)),
            pltpu.SemaphoreType.DMA((2 + CHUNKS, 3, patches)),
            pltpu.SemaphoreType.DMA((2 + CHUNKS, patches)),
            pltpu.SemaphoreType.DMA((experts,)),
            pltpu.SemaphoreType.DMA((2, experts)),
            pltpu.SemaphoreType.DMA((CHUNKS, 2, experts)),
            pltpu.SemaphoreType.DMA((CHUNKS, experts)),
        ],
        compiler_params=pltpu.CompilerParams(
            collective_id=0, has_side_effects=True, vmem_limit_bytes=56 * 1024 * 1024
        ),
    )(
        latent[0], stale_kv[0], jnp.transpose(modulation, (1, 0, 2)), routes[0, 0].T, w_qkv.T,
        w_attn_out, router.T, w_in[0], w_out[0],
    )
    return (state[None], current[None])


def solution(mesh):
    line_of_four = mesh.shape["patch"] == 8 and mesh.shape["expert"] == 4
    in_specs = (
        P("expert", "patch", None),
        P("expert", "patch", None),
        P(),
        P(None, "expert", "patch", None),
        P(),
        P(),
        P(),
        P("expert", "patch", None),
        P("expert", "patch", None),
    )
    out_specs = (P("expert", "patch", None), P("expert", "patch", None))
    return jax.shard_map(
        on_line if line_of_four else on_device, mesh=mesh, in_specs=in_specs, out_specs=out_specs, check_vma=False
    )
```

```python
import functools

import jax
import jax.numpy as jnp
from jax import lax
from jax.experimental import pallas as pl
from jax.experimental.pallas import tpu as pltpu
from jax.sharding import PartitionSpec as P

HEADS = 8


EPSILON = 1e-06


def normalize(values, shift, scale):
    widened = values.astype(jnp.float32)
    center = jnp.mean(widened, axis=-1, keepdims=True)
    spread = jnp.mean(jnp.square(widened - center), axis=-1, keepdims=True)
    return ((widened - center) * lax.rsqrt(spread + EPSILON) * (1.0 + scale) + shift).astype(
        jnp.bfloat16
    )


def attend_keys(query, current, previous, own_start, head_count):
    token_count, attn_width = query.shape
    head_size = attn_width // head_count
    factor = head_size ** (-0.5)
    query_heads = query.reshape(token_count, head_count, head_size)

    def scores_of(kv_rows):
        keys = kv_rows[:, :attn_width].reshape(kv_rows.shape[0], head_count, head_size)
        return (
            jnp.einsum("qhd,khd->hqk", query_heads, keys, preferred_element_type=jnp.float32)
            * factor
        )

    def values_of(kv_rows):
        return kv_rows[:, attn_width:].reshape(kv_rows.shape[0], head_count, head_size)

    own_scores = scores_of(current)
    highest = jnp.max(own_scores, axis=-1)
    weights = jnp.exp(own_scores - highest[..., None])
    totals = jnp.sum(weights, axis=-1)
    summed = jnp.einsum(
        "hqk,khd->hqd",
        weights.astype(jnp.bfloat16),
        values_of(current),
        preferred_element_type=jnp.float32,
    )
    best = highest
    mass = totals
    accum = summed
    rows = lax.all_gather(previous[None], "patch", axis=1, tiled=True)[0]
    positions = jnp.arange(rows.shape[0], dtype=jnp.int32)
    foreign = (positions < own_start) | (positions >= own_start + token_count)
    scores = jnp.where(foreign[None, None, :], scores_of(rows), -1e30)
    renewed = jnp.maximum(best, jnp.max(scores, axis=-1))
    decay = jnp.exp(best - renewed)
    fresh = jnp.exp(scores - renewed[..., None])
    mass = mass * decay + jnp.sum(fresh, axis=-1)
    added = jnp.einsum(
        "hqk,khd->hqd",
        fresh.astype(jnp.bfloat16),
        values_of(rows),
        preferred_element_type=jnp.float32,
    )
    best, mass, accum = (renewed, mass, accum * decay[..., None] + added)
    result = accum / mass[..., None]
    return jnp.transpose(result, (1, 0, 2)).reshape(token_count, attn_width).astype(jnp.bfloat16)


def expert_block(normed, chosen, router, weight_in, weight_out, capacity):
    token_count, width = normed.shape
    expert_count = router.shape[1]
    logits = jnp.dot(normed, router, preferred_element_type=jnp.float32)
    onehot = chosen[..., None] == jnp.arange(expert_count, dtype=jnp.int32)
    gates = jax.nn.sigmoid(jnp.sum(jnp.where(onehot, logits[:, None, :], 0.0), axis=-1))
    flat = onehot.reshape(2 * token_count, expert_count).astype(jnp.int32)
    slots = jnp.sum((jnp.cumsum(flat, axis=0) - flat) * flat, axis=-1)
    targets = chosen.reshape(-1) * capacity + slots
    columns = jnp.arange(expert_count * capacity, dtype=jnp.int32)
    placement = jnp.sum(
        (targets.reshape(token_count, 2)[:, :, None] == columns[None, None, :]).astype(
            jnp.bfloat16
        ),
        axis=1,
    )
    outgoing = jnp.einsum(
        "ts,td->sd", placement, normed, preferred_element_type=jnp.float32
    ).astype(jnp.bfloat16)
    outgoing = outgoing.reshape(expert_count, capacity, width)
    arrived = lax.all_to_all(outgoing, "expert", split_axis=0, concat_axis=0, tiled=True)
    flat_rows = arrived.reshape(expert_count * capacity, width)
    hidden = jax.nn.gelu(
        jnp.dot(flat_rows, weight_in, preferred_element_type=jnp.float32), approximate=True
    ).astype(jnp.bfloat16)
    produced = jnp.dot(hidden, weight_out, preferred_element_type=jnp.float32).astype(jnp.bfloat16)
    returned = lax.all_to_all(
        produced.reshape(expert_count, capacity, width),
        "expert",
        split_axis=0,
        concat_axis=0,
        tiled=True,
    )
    picked = (
        returned.reshape(expert_count * capacity, width)[targets]
        .astype(jnp.float32)
        .reshape(token_count, 2, width)
    )
    return jnp.sum(picked * gates[..., None], axis=1)


def on_device(latent, stale_kv, modulation, routes, w_qkv, w_attn_out, router, w_in, w_out):
    token_count = latent.shape[1]
    attn_width = w_attn_out.shape[0]
    expert_groups = lax.axis_size("expert")
    capacity = min(token_count, 5 * token_count // (2 * expert_groups))
    full_in, full_out = (
        lax.all_gather(w_in, "patch", axis=1, tiled=True),
        lax.all_gather(w_out, "patch", axis=1, tiled=True),
    )
    full_in = full_in[0]
    full_out = full_out[0]
    own_start = lax.axis_index("patch") * token_count
    state = latent[0]
    previous = stale_kv[0]
    shifts = modulation[0]
    normed = normalize(state, shifts[0], shifts[1])
    merged = jnp.dot(normed, w_qkv, preferred_element_type=jnp.float32).astype(jnp.bfloat16)
    query = merged[:, :attn_width]
    current = merged[:, attn_width:]
    attended = attend_keys(query, current, previous, own_start, HEADS)
    projected = jnp.dot(attended, w_attn_out, preferred_element_type=jnp.float32)
    middle = (state.astype(jnp.float32) + shifts[2] * projected).astype(jnp.bfloat16)
    normed_two = normalize(middle, shifts[3], shifts[4])
    mixture = expert_block(normed_two, routes[0, 0], router, full_in, full_out, capacity)
    state = (middle.astype(jnp.float32) + shifts[5] * mixture).astype(jnp.bfloat16)
    return (state[None], current[None])


MESH = pl.DeviceIdType.MESH
TO_PARTNER, TO_MIDDLE, TO_CORE = 0, 1, 2
CHUNKS = 3


def block_kernel(
    capacity,
    latent_ref, stale_ref, mod_ref, routes_ref, wqkv_hbm, wattn_hbm, router_ref, win_hbm, wout_hbm,
    out_ref, fresh_ref,
    kv, wqkv, wattn, win, wout, outgoing, rows, hidden, produced, returned, attended,
    load_sem, send_sem, recv_sem, go_send, go_recv, back_send, back_recv,
):
    patch, expert = lax.axis_index("patch"), lax.axis_index("expert")
    z, core = patch // 2, patch % 2
    other = z * 2 + (1 - core)
    partner = (z + 1 - 2 * (z % 2)) * 2 + core
    across = (3 - z) * 2 + core
    far = (3 - partner // 2) * 2 + core
    middle_plane = (z == 1) | (z == 2)
    end_plane = (z == 0) | (z == 3)
    tokens, width = latent_ref.shape
    attn = wattn_hbm.shape[0]
    head_size = attn // HEADS
    experts = router_ref.shape[0]
    ffw = win_hbm.shape[1]

    chunk = width // CHUNKS
    chunks = range(2, 2 + CHUNKS)
    buffers = [kv, win] + [wout.at[part] for part in range(CHUNKS)]
    owned = [stale_ref, win_hbm] + [
        wout_hbm.at[:, pl.ds(part * chunk, chunk)] for part in range(CHUNKS)
    ]

    def slot(which, index):
        count = owned[which].shape[0]
        return buffers[which].at[pl.ds(pl.multiple_of(index * count, 16), count)]

    def transfer(which, kind, index, own=False):
        target = (partner, across, other)[kind]
        return pltpu.make_async_remote_copy(
            src_ref=owned[which] if own else slot(which, index),
            dst_ref=slot(which, index),
            send_sem=send_sem.at[which, kind, index],
            recv_sem=recv_sem.at[which, index],
            device_id=(target, expert),
            device_id_type=MESH,
        )

    def arrived(which, index):
        transfer(which, TO_CORE, index).wait_recv()

    load_qkv = pltpu.make_async_copy(wqkv_hbm, wqkv, load_sem.at[0])
    load_attn = pltpu.make_async_copy(
        wattn_hbm, wattn.at[pl.ds(wattn.shape[0] - attn, attn)], load_sem.at[1]
    )
    load_qkv.start()
    load_attn.start()
    own_loads = [
        pltpu.make_async_copy(owned[which], slot(which, patch), load_sem.at[1 + which])
        for which in range(1, 2 + CHUNKS)
    ]

    @pl.when(middle_plane)
    def _():
        for load in own_loads:
            load.start()

    barrier = pltpu.get_barrier_semaphore()
    peers = [(other, expert), (partner, expert), (across, expert)]
    for step in range(1, experts):
        peers.append((patch, (expert + step) % experts))
        peers.append((partner, (expert + step) % experts))
    for peer in peers:
        pl.semaphore_signal(barrier, inc=1, device_id=peer, device_id_type=MESH)
    pl.semaphore_wait(barrier, len(peers))

    transfer(0, TO_PARTNER, patch, True).start()
    transfer(0, TO_CORE, patch, True).start()

    @pl.when(middle_plane)
    def _():
        transfer(0, TO_MIDDLE, patch, True).start()

    def row_of(index):
        return mod_ref[index]

    def times_rows(left, right):
        return lax.dot_general(
            left, right, (((1,), (1,)), ((), ())), preferred_element_type=jnp.float32
        )

    normed = normalize(latent_ref[...], row_of(0), row_of(1))
    load_qkv.wait()
    query = times_rows(normed, wqkv[: wattn.shape[0], :]).astype(jnp.bfloat16)
    current = times_rows(normed, wqkv[attn:, :]).astype(jnp.bfloat16)
    fresh_ref[...] = current
    kv[pl.ds(pl.multiple_of(patch * tokens, 16), tokens), :] = current

    @pl.when(middle_plane)
    def _():
        arrived(0, partner)
        transfer(0, TO_MIDDLE, partner).start()
        transfer(0, TO_CORE, partner).start()
        transfer(1, TO_MIDDLE, patch, True).start()
        arrived(0, across)
        transfer(0, TO_PARTNER, across).start()
        transfer(0, TO_CORE, across).start()
        arrived(0, far)
        transfer(0, TO_PARTNER, far).start()
        transfer(0, TO_CORE, far).start()
        transfer(2, TO_MIDDLE, patch, True).start()

    @pl.when(end_plane)
    def _():
        transfer(0, TO_PARTNER, patch, True).wait_send()
        transfer(1, TO_PARTNER, patch, True).start()
        transfer(2, TO_PARTNER, patch, True).start()
        for index in (partner, across, far):
            arrived(0, index)
            transfer(0, TO_CORE, index).start()

    for plane in range(4):
        arrived(0, plane * 2 + 1 - core)

    lead = wattn.shape[0] - attn
    base = attn - lead
    for head in range(HEADS):
        low, high = head * head_size, (head + 1) * head_size
        start, stop = low // 128 * 128, -(-high // 128) * 128
        column = lax.broadcasted_iota(jnp.int32, (tokens, stop - start), 1) + start
        chosen = jnp.where(
            (column >= low) & (column < high), query[:, start:stop].astype(jnp.float32), 0.0
        ).astype(jnp.bfloat16)
        scores = times_rows(chosen, kv[:, start:stop]) * head_size ** (-0.5)
        weights = jnp.exp(scores - jnp.max(scores, axis=-1, keepdims=True))
        total = jnp.sum(weights, axis=-1, keepdims=True)
        low, high = attn + low, attn + high
        start, stop = low // 128 * 128, -(-high // 128) * 128
        summed = (
            jnp.dot(
                weights.astype(jnp.bfloat16), kv[:, start:stop], preferred_element_type=jnp.float32
            )
            / total
        )
        column = lax.broadcasted_iota(jnp.int32, (tokens, stop - start), 1) + start
        mine = jnp.where((column >= low) & (column < high), summed, 0.0)
        first = start - base
        old = attended[:, first : first + stop - start]
        keep = (column < low) & (column >= attn)
        attended[:, first : first + stop - start] = jnp.where(keep, old, mine)
        if head == HEADS // 2 - 1:

            @pl.when(middle_plane)
            def _():
                arrived(1, partner)
                transfer(1, TO_MIDDLE, partner).start()
                transfer(1, TO_CORE, partner).start()
                transfer(1, TO_CORE, patch, True).start()

            @pl.when(end_plane)
            def _():
                transfer(3, TO_PARTNER, patch, True).start()
                transfer(4, TO_PARTNER, patch, True).start()

    @pl.when(middle_plane)
    def _():
        arrived(2, partner)
        transfer(2, TO_MIDDLE, partner).start()
        transfer(3, TO_MIDDLE, patch, True).start()

    load_attn.wait()
    wattn[:lead, :] = jnp.zeros((lead, width), jnp.bfloat16)
    projected = jnp.dot(
        attended[...].astype(jnp.bfloat16), wattn[...], preferred_element_type=jnp.float32
    )
    middle = (latent_ref[...].astype(jnp.float32) + row_of(2) * projected).astype(jnp.bfloat16)
    out_ref[...] = middle
    normed_two = normalize(middle, row_of(3), row_of(4))
    logits = times_rows(normed_two, router_ref[...])

    line = lax.broadcasted_iota(jnp.int32, (tokens, tokens), 0)
    lane = lax.broadcasted_iota(jnp.int32, (tokens, tokens), 1)
    named = ((routes_ref[0:1, :] == line) | (routes_ref[1:2, :] == line)).astype(jnp.float32)
    place_t = jnp.dot(
        named.astype(jnp.bfloat16),
        (line < lane).astype(jnp.float32).astype(jnp.bfloat16),
        preferred_element_type=jnp.float32,
    )
    place_t = jnp.where(named > 0.0, place_t, -1.0)
    place = place_t.T
    entry = lax.broadcasted_iota(jnp.int32, (capacity, tokens), 0).astype(jnp.float32)
    for index in range(experts):
        pick = (entry == place_t[index : index + 1, :]).astype(jnp.float32).astype(jnp.bfloat16)
        outgoing[index * capacity : (index + 1) * capacity, :] = jnp.dot(
            pick, normed_two, preferred_element_type=jnp.float32
        ).astype(jnp.bfloat16)

    def span(index):
        return pl.ds(pl.multiple_of(index * capacity, 16), capacity)

    def go(side, index):
        return pltpu.make_async_remote_copy(
            src_ref=outgoing.at[span(index)],
            dst_ref=rows.at[span(side * experts + expert)],
            send_sem=go_send.at[index],
            recv_sem=go_recv.at[side, expert],
            device_id=(partner if side else patch, index),
            device_id_type=MESH,
        )

    def back(side, index, part):
        return pltpu.make_async_remote_copy(
            src_ref=produced.at[part, span(side * experts + index)],
            dst_ref=returned.at[part, span(expert)],
            send_sem=back_send.at[part, side, index],
            recv_sem=back_recv.at[part, expert],
            device_id=(partner if side else patch, index),
            device_id_type=MESH,
        )

    def await_rows(side, source):
        pltpu.make_async_copy(
            outgoing.at[span(source)],
            rows.at[span(side * experts + source)],
            go_recv.at[side, source],
        ).wait()

    def await_back(source, part):
        pltpu.make_async_copy(
            produced.at[part, span(source)],
            returned.at[part, span(source)],
            back_recv.at[part, source],
        ).wait()

    @pl.when(end_plane)
    def _():
        for step in range(experts):
            go(1, (expert + step) % experts).start()

    @pl.when(middle_plane)
    def _():
        for step in range(1, experts):
            go(0, (expert + step) % experts).start()
        rows[span(expert), :] = outgoing[span(expert), :]
        for which in chunks[1:]:
            arrived(which, partner)
            transfer(which, TO_MIDDLE, partner).start()
            if which + 1 in chunks:
                transfer(which + 1, TO_MIDDLE, patch, True).start()
        for index in (across, far):
            arrived(1, index)
            transfer(1, TO_CORE, index).start()
        for which in chunks:
            transfer(which, TO_CORE, patch, True).start()
            transfer(which, TO_CORE, partner).start()
        for load in own_loads:
            load.wait()
        for step in range(1, experts):
            await_rows(0, (expert + step) % experts)
        for step in range(experts):
            await_rows(1, (expert + step) % experts)
        for plane in range(4):
            arrived(1, plane * 2 + 1 - core)

        def first_layer(step, carry):
            columns = pl.ds(pl.multiple_of(step * 256, 256), 256)
            hidden[:, columns] = jax.nn.gelu(
                jnp.dot(rows[...], win[:, columns], preferred_element_type=jnp.float32),
                approximate=True,
            ).astype(jnp.bfloat16)
            return carry

        lax.fori_loop(0, ffw // 256, first_layer, 0)

        count = experts * capacity
        for part in range(CHUNKS):
            which = part + 2
            for index in (across, far):
                arrived(which, index)
                transfer(which, TO_CORE, index).start()
            for plane in range(4):
                arrived(which, plane * 2 + 1 - core)
            for side in (1, 0):
                block = slice(side * count, (side + 1) * count)
                produced[part, block, :] = jnp.dot(
                    hidden[block, :], wout[part], preferred_element_type=jnp.float32
                ).astype(jnp.bfloat16)
                for step in range(1 - side, experts):
                    back(side, (expert + step) % experts, part).start()
            returned[part, span(expert), :] = produced[part, span(expert), :]

    entry = lax.broadcasted_iota(jnp.int32, (tokens, capacity), 1).astype(jnp.float32)
    gates = jax.nn.sigmoid(logits)
    picks = [
        (entry == place[:, index : index + 1]).astype(jnp.float32).astype(jnp.bfloat16)
        for index in range(experts)
    ]
    for part in range(CHUNKS):
        for step in range(1, experts):
            await_back((expert + step) % experts, part)

        @pl.when(end_plane)
        def _():
            await_back(expert, part)

        columns = slice(part * chunk, (part + 1) * chunk)
        mixture = jnp.zeros((tokens, chunk), jnp.float32)
        for index in range(experts):
            picked = jnp.dot(
                picks[index],
                returned[part, index * capacity : (index + 1) * capacity, :],
                preferred_element_type=jnp.float32,
            )
            mixture = mixture + picked * gates[:, index : index + 1]
        out_ref[:, columns] = (
            out_ref[:, columns].astype(jnp.float32) + row_of(5)[:, columns] * mixture
        ).astype(jnp.bfloat16)

    transfer(0, TO_CORE, patch, True).wait_send()
    for index in (partner, across, far):
        transfer(0, TO_CORE, index).wait_send()

    @pl.when(end_plane)
    def _():
        for which in range(1, 2 + CHUNKS):
            transfer(which, TO_PARTNER, patch, True).wait_send()
        for step in range(experts):
            go(1, (expert + step) % experts).wait_send()

    @pl.when(middle_plane)
    def _():
        transfer(0, TO_PARTNER, patch, True).wait_send()
        transfer(0, TO_MIDDLE, patch, True).wait_send()
        transfer(0, TO_MIDDLE, partner).wait_send()
        transfer(0, TO_PARTNER, across).wait_send()
        transfer(0, TO_PARTNER, far).wait_send()
        for which in range(1, 2 + CHUNKS):
            transfer(which, TO_MIDDLE, patch, True).wait_send()
            transfer(which, TO_MIDDLE, partner).wait_send()
            transfer(which, TO_CORE, patch, True).wait_send()
            for index in (partner, across, far):
                transfer(which, TO_CORE, index).wait_send()
        for step in range(1, experts):
            go(0, (expert + step) % experts).wait_send()
        for part in range(CHUNKS):
            for side in (1, 0):
                for step in range(1 - side, experts):
                    back(side, (expert + step) % experts, part).wait_send()


def store_kernel(state_ref, current_ref, out_ref, fresh_ref):
    out_ref[...] = state_ref[...]
    fresh_ref[...] = current_ref[...]


def on_line(latent, stale_kv, modulation, routes, w_qkv, w_attn_out, router, w_in, w_out):
    tokens, width = latent.shape[1:]
    attn = w_attn_out.shape[0]
    experts, patches = lax.axis_size("expert"), lax.axis_size("patch")
    capacity = min(tokens, 5 * tokens // (2 * experts))
    ffw = w_in.shape[2]
    padded = -(-attn // 128) * 128
    slots = experts * capacity
    vmem, hbm = pl.BlockSpec(memory_space=pltpu.VMEM), pl.BlockSpec(memory_space=pl.ANY)
    narrow = jnp.bfloat16
    state, current = pl.pallas_call(
        functools.partial(block_kernel, capacity),
        out_shape=(
            jax.ShapeDtypeStruct((tokens, width), narrow),
            jax.ShapeDtypeStruct((tokens, 2 * attn), narrow),
        ),
        in_specs=[vmem, hbm, vmem, vmem, hbm, hbm, vmem, hbm, hbm],
        out_specs=(vmem, vmem),
        scratch_shapes=[
            pltpu.VMEM((patches * tokens, 2 * attn), narrow),
            pltpu.VMEM(w_qkv.shape[::-1], narrow),
            pltpu.VMEM((padded, width), narrow),
            pltpu.VMEM((width, ffw), narrow),
            pltpu.VMEM((CHUNKS, ffw, width // CHUNKS), narrow),
            pltpu.VMEM((slots, width), narrow),
            pltpu.VMEM((2 * slots, width), narrow),
            pltpu.VMEM((2 * slots, ffw), narrow),
            pltpu.VMEM((CHUNKS, 2 * slots, width // CHUNKS), narrow),
            pltpu.VMEM((CHUNKS, slots, width // CHUNKS), narrow),
            pltpu.VMEM((tokens, padded), jnp.float32),
            pltpu.SemaphoreType.DMA((3 + CHUNKS,)),
            pltpu.SemaphoreType.DMA((2 + CHUNKS, 3, patches)),
            pltpu.SemaphoreType.DMA((2 + CHUNKS, patches)),
            pltpu.SemaphoreType.DMA((experts,)),
            pltpu.SemaphoreType.DMA((2, experts)),
            pltpu.SemaphoreType.DMA((CHUNKS, 2, experts)),
            pltpu.SemaphoreType.DMA((CHUNKS, experts)),
        ],
        compiler_params=pltpu.CompilerParams(
            collective_id=0, has_side_effects=True, vmem_limit_bytes=56 * 1024 * 1024
        ),
    )(
        latent[0], stale_kv[0], jnp.transpose(modulation, (1, 0, 2)), routes[0, 0].T, w_qkv.T,
        w_attn_out, router.T, w_in[0], w_out[0],
    )
    state, current = pl.pallas_call(
        store_kernel,
        out_shape=(
            jax.ShapeDtypeStruct(state.shape, narrow),
            jax.ShapeDtypeStruct(current.shape, narrow),
        ),
        in_specs=[vmem, vmem],
        out_specs=(vmem, vmem),
    )(state, current)
    return (state[None], current[None])


def solution(mesh):
    line_of_four = mesh.shape["patch"] == 8 and mesh.shape["expert"] == 4
    in_specs = (
        P("expert", "patch", None),
        P("expert", "patch", None),
        P(),
        P(None, "expert", "patch", None),
        P(),
        P(),
        P(),
        P("expert", "patch", None),
        P("expert", "patch", None),
    )
    out_specs = (P("expert", "patch", None), P("expert", "patch", None))
    return jax.shard_map(
        on_line if line_of_four else on_device, mesh=mesh, in_specs=in_specs, out_specs=out_specs, check_vma=False
    )
```

```python
import functools

import jax
import jax.numpy as jnp
from jax import lax
from jax.experimental import pallas as pl
from jax.experimental.pallas import tpu as pltpu
from jax.sharding import PartitionSpec as P

HEADS = 8


EPSILON = 1e-06


def normalize(values, shift, scale):
    widened = values.astype(jnp.float32)
    center = jnp.mean(widened, axis=-1, keepdims=True)
    spread = jnp.mean(jnp.square(widened - center), axis=-1, keepdims=True)
    return ((widened - center) * lax.rsqrt(spread + EPSILON) * (1.0 + scale) + shift).astype(
        jnp.bfloat16
    )


def attend_keys(query, current, previous, own_start, head_count):
    token_count, attn_width = query.shape
    head_size = attn_width // head_count
    factor = head_size ** (-0.5)
    query_heads = query.reshape(token_count, head_count, head_size)

    def scores_of(kv_rows):
        keys = kv_rows[:, :attn_width].reshape(kv_rows.shape[0], head_count, head_size)
        return (
            jnp.einsum("qhd,khd->hqk", query_heads, keys, preferred_element_type=jnp.float32)
            * factor
        )

    def values_of(kv_rows):
        return kv_rows[:, attn_width:].reshape(kv_rows.shape[0], head_count, head_size)

    own_scores = scores_of(current)
    highest = jnp.max(own_scores, axis=-1)
    weights = jnp.exp(own_scores - highest[..., None])
    totals = jnp.sum(weights, axis=-1)
    summed = jnp.einsum(
        "hqk,khd->hqd",
        weights.astype(jnp.bfloat16),
        values_of(current),
        preferred_element_type=jnp.float32,
    )
    best = highest
    mass = totals
    accum = summed
    rows = lax.all_gather(previous[None], "patch", axis=1, tiled=True)[0]
    positions = jnp.arange(rows.shape[0], dtype=jnp.int32)
    foreign = (positions < own_start) | (positions >= own_start + token_count)
    scores = jnp.where(foreign[None, None, :], scores_of(rows), -1e30)
    renewed = jnp.maximum(best, jnp.max(scores, axis=-1))
    decay = jnp.exp(best - renewed)
    fresh = jnp.exp(scores - renewed[..., None])
    mass = mass * decay + jnp.sum(fresh, axis=-1)
    added = jnp.einsum(
        "hqk,khd->hqd",
        fresh.astype(jnp.bfloat16),
        values_of(rows),
        preferred_element_type=jnp.float32,
    )
    best, mass, accum = (renewed, mass, accum * decay[..., None] + added)
    result = accum / mass[..., None]
    return jnp.transpose(result, (1, 0, 2)).reshape(token_count, attn_width).astype(jnp.bfloat16)


def expert_block(normed, chosen, router, weight_in, weight_out, capacity):
    token_count, width = normed.shape
    expert_count = router.shape[1]
    logits = jnp.dot(normed, router, preferred_element_type=jnp.float32)
    onehot = chosen[..., None] == jnp.arange(expert_count, dtype=jnp.int32)
    gates = jax.nn.sigmoid(jnp.sum(jnp.where(onehot, logits[:, None, :], 0.0), axis=-1))
    flat = onehot.reshape(2 * token_count, expert_count).astype(jnp.int32)
    slots = jnp.sum((jnp.cumsum(flat, axis=0) - flat) * flat, axis=-1)
    targets = chosen.reshape(-1) * capacity + slots
    columns = jnp.arange(expert_count * capacity, dtype=jnp.int32)
    placement = jnp.sum(
        (targets.reshape(token_count, 2)[:, :, None] == columns[None, None, :]).astype(
            jnp.bfloat16
        ),
        axis=1,
    )
    outgoing = jnp.einsum(
        "ts,td->sd", placement, normed, preferred_element_type=jnp.float32
    ).astype(jnp.bfloat16)
    outgoing = outgoing.reshape(expert_count, capacity, width)
    arrived = lax.all_to_all(outgoing, "expert", split_axis=0, concat_axis=0, tiled=True)
    flat_rows = arrived.reshape(expert_count * capacity, width)
    hidden = jax.nn.gelu(
        jnp.dot(flat_rows, weight_in, preferred_element_type=jnp.float32), approximate=True
    ).astype(jnp.bfloat16)
    produced = jnp.dot(hidden, weight_out, preferred_element_type=jnp.float32).astype(jnp.bfloat16)
    returned = lax.all_to_all(
        produced.reshape(expert_count, capacity, width),
        "expert",
        split_axis=0,
        concat_axis=0,
        tiled=True,
    )
    picked = (
        returned.reshape(expert_count * capacity, width)[targets]
        .astype(jnp.float32)
        .reshape(token_count, 2, width)
    )
    return jnp.sum(picked * gates[..., None], axis=1)


def on_device(latent, stale_kv, modulation, routes, w_qkv, w_attn_out, router, w_in, w_out):
    token_count = latent.shape[1]
    attn_width = w_attn_out.shape[0]
    expert_groups = lax.axis_size("expert")
    capacity = min(token_count, 5 * token_count // (2 * expert_groups))
    full_in, full_out = (
        lax.all_gather(w_in, "patch", axis=1, tiled=True),
        lax.all_gather(w_out, "patch", axis=1, tiled=True),
    )
    full_in = full_in[0]
    full_out = full_out[0]
    own_start = lax.axis_index("patch") * token_count
    state = latent[0]
    previous = stale_kv[0]
    shifts = modulation[0]
    normed = normalize(state, shifts[0], shifts[1])
    merged = jnp.dot(normed, w_qkv, preferred_element_type=jnp.float32).astype(jnp.bfloat16)
    query = merged[:, :attn_width]
    current = merged[:, attn_width:]
    attended = attend_keys(query, current, previous, own_start, HEADS)
    projected = jnp.dot(attended, w_attn_out, preferred_element_type=jnp.float32)
    middle = (state.astype(jnp.float32) + shifts[2] * projected).astype(jnp.bfloat16)
    normed_two = normalize(middle, shifts[3], shifts[4])
    mixture = expert_block(normed_two, routes[0, 0], router, full_in, full_out, capacity)
    state = (middle.astype(jnp.float32) + shifts[5] * mixture).astype(jnp.bfloat16)
    return (state[None], current[None])


MESH = pl.DeviceIdType.MESH
TO_PARTNER, TO_MIDDLE, TO_CORE = 0, 1, 2
CHUNKS = 3


def block_kernel(
    capacity,
    latent_ref, stale_ref, mod_ref, routes_ref, wqkv_hbm, wattn_hbm, router_ref, win_hbm, wout_hbm,
    out_ref, fresh_ref,
    kv, wqkv, wattn, win, wout, outgoing, rows, hidden, produced, returned, attended,
    load_sem, send_sem, recv_sem, go_send, go_recv, back_send, back_recv,
):
    patch, expert = lax.axis_index("patch"), lax.axis_index("expert")
    z, core = patch // 2, patch % 2
    other = z * 2 + (1 - core)
    partner = (z + 1 - 2 * (z % 2)) * 2 + core
    across = (3 - z) * 2 + core
    far = (3 - partner // 2) * 2 + core
    middle_plane = (z == 1) | (z == 2)
    end_plane = (z == 0) | (z == 3)
    tokens, width = latent_ref.shape
    attn = wattn_hbm.shape[0]
    head_size = attn // HEADS
    experts = router_ref.shape[0]
    ffw = win_hbm.shape[1]

    chunk = width // CHUNKS
    chunks = range(2, 2 + CHUNKS)
    buffers = [kv, win] + [wout.at[part] for part in range(CHUNKS)]
    owned = [stale_ref, win_hbm] + [
        wout_hbm.at[:, pl.ds(part * chunk, chunk)] for part in range(CHUNKS)
    ]

    def slot(which, index):
        count = owned[which].shape[0]
        return buffers[which].at[pl.ds(pl.multiple_of(index * count, 16), count)]

    def transfer(which, kind, index, own=False):
        target = (partner, across, other)[kind]
        return pltpu.make_async_remote_copy(
            src_ref=owned[which] if own else slot(which, index),
            dst_ref=slot(which, index),
            send_sem=send_sem.at[which, kind, index],
            recv_sem=recv_sem.at[which, index],
            device_id=(target, expert),
            device_id_type=MESH,
        )

    def arrived(which, index):
        transfer(which, TO_CORE, index).wait_recv()

    load_qkv = pltpu.make_async_copy(wqkv_hbm, wqkv, load_sem.at[0])
    load_attn = pltpu.make_async_copy(
        wattn_hbm, wattn.at[pl.ds(wattn.shape[0] - attn, attn)], load_sem.at[1]
    )
    load_qkv.start()
    load_attn.start()
    own_loads = [
        pltpu.make_async_copy(owned[which], slot(which, patch), load_sem.at[1 + which])
        for which in range(1, 2 + CHUNKS)
    ]

    @pl.when(middle_plane)
    def _():
        for load in own_loads:
            load.start()

    barrier = pltpu.get_barrier_semaphore()
    peers = [(other, expert), (partner, expert), (across, expert)]
    for step in range(1, experts):
        peers.append((patch, (expert + step) % experts))
        peers.append((partner, (expert + step) % experts))
    for peer in peers:
        pl.semaphore_signal(barrier, inc=1, device_id=peer, device_id_type=MESH)
    pl.semaphore_wait(barrier, len(peers))

    transfer(0, TO_PARTNER, patch, True).start()
    transfer(0, TO_CORE, patch, True).start()

    @pl.when(middle_plane)
    def _():
        transfer(0, TO_MIDDLE, patch, True).start()

    def row_of(index):
        return mod_ref[index]

    def times_rows(left, right):
        return lax.dot_general(
            left, right, (((1,), (1,)), ((), ())), preferred_element_type=jnp.float32
        )

    normed = normalize(latent_ref[...], row_of(0), row_of(1))
    load_qkv.wait()
    query = times_rows(normed, wqkv[: wattn.shape[0], :]).astype(jnp.bfloat16)
    current = times_rows(normed, wqkv[attn:, :]).astype(jnp.bfloat16)
    fresh_ref[...] = current
    kv[pl.ds(pl.multiple_of(patch * tokens, 16), tokens), :] = current

    @pl.when(middle_plane)
    def _():
        arrived(0, partner)
        transfer(0, TO_MIDDLE, partner).start()
        transfer(0, TO_CORE, partner).start()
        transfer(1, TO_MIDDLE, patch, True).start()
        arrived(0, across)
        transfer(0, TO_PARTNER, across).start()
        transfer(0, TO_CORE, across).start()
        arrived(0, far)
        transfer(0, TO_PARTNER, far).start()
        transfer(0, TO_CORE, far).start()
        transfer(2, TO_MIDDLE, patch, True).start()

    @pl.when(end_plane)
    def _():
        transfer(0, TO_PARTNER, patch, True).wait_send()
        transfer(1, TO_PARTNER, patch, True).start()
        transfer(2, TO_PARTNER, patch, True).start()
        for index in (partner, across, far):
            arrived(0, index)
            transfer(0, TO_CORE, index).start()

    for plane in range(4):
        arrived(0, plane * 2 + 1 - core)

    lead = wattn.shape[0] - attn
    base = attn - lead
    for head in range(HEADS):
        low, high = head * head_size, (head + 1) * head_size
        start, stop = low // 128 * 128, -(-high // 128) * 128
        column = lax.broadcasted_iota(jnp.int32, (tokens, stop - start), 1) + start
        chosen = jnp.where(
            (column >= low) & (column < high), query[:, start:stop].astype(jnp.float32), 0.0
        ).astype(jnp.bfloat16)
        scores = times_rows(chosen, kv[:, start:stop]) * head_size ** (-0.5)
        weights = jnp.exp(scores - jnp.max(scores, axis=-1, keepdims=True))
        total = jnp.sum(weights, axis=-1, keepdims=True)
        low, high = attn + low, attn + high
        start, stop = low // 128 * 128, -(-high // 128) * 128
        summed = (
            jnp.dot(
                weights.astype(jnp.bfloat16), kv[:, start:stop], preferred_element_type=jnp.float32
            )
            / total
        )
        column = lax.broadcasted_iota(jnp.int32, (tokens, stop - start), 1) + start
        mine = jnp.where((column >= low) & (column < high), summed, 0.0)
        first = start - base
        old = attended[:, first : first + stop - start]
        keep = (column < low) & (column >= attn)
        attended[:, first : first + stop - start] = jnp.where(keep, old, mine)
        if head == HEADS // 2 - 1:

            @pl.when(middle_plane)
            def _():
                arrived(1, partner)
                transfer(1, TO_MIDDLE, partner).start()
                transfer(1, TO_CORE, partner).start()
                transfer(1, TO_CORE, patch, True).start()

            @pl.when(end_plane)
            def _():
                transfer(3, TO_PARTNER, patch, True).start()
                transfer(4, TO_PARTNER, patch, True).start()

    @pl.when(middle_plane)
    def _():
        arrived(2, partner)
        transfer(2, TO_MIDDLE, partner).start()
        transfer(3, TO_MIDDLE, patch, True).start()

    load_attn.wait()
    wattn[:lead, :] = jnp.zeros((lead, width), jnp.bfloat16)
    projected = jnp.dot(
        attended[...].astype(jnp.bfloat16), wattn[...], preferred_element_type=jnp.float32
    )
    middle = (latent_ref[...].astype(jnp.float32) + row_of(2) * projected).astype(jnp.bfloat16)
    out_ref[...] = middle
    normed_two = normalize(middle, row_of(3), row_of(4))
    logits = times_rows(normed_two, router_ref[...])

    line = lax.broadcasted_iota(jnp.int32, (tokens, tokens), 0)
    lane = lax.broadcasted_iota(jnp.int32, (tokens, tokens), 1)
    named = ((routes_ref[0:1, :] == line) | (routes_ref[1:2, :] == line)).astype(jnp.float32)
    place_t = jnp.dot(
        named.astype(jnp.bfloat16),
        (line < lane).astype(jnp.float32).astype(jnp.bfloat16),
        preferred_element_type=jnp.float32,
    )
    place_t = jnp.where(named > 0.0, place_t, -1.0)
    place = place_t.T
    entry = lax.broadcasted_iota(jnp.int32, (capacity, tokens), 0).astype(jnp.float32)
    for index in range(experts):
        pick = (entry == place_t[index : index + 1, :]).astype(jnp.float32).astype(jnp.bfloat16)
        outgoing[index * capacity : (index + 1) * capacity, :] = jnp.dot(
            pick, normed_two, preferred_element_type=jnp.float32
        ).astype(jnp.bfloat16)

    def span(index):
        return pl.ds(pl.multiple_of(index * capacity, 16), capacity)

    def go(side, index):
        return pltpu.make_async_remote_copy(
            src_ref=outgoing.at[span(index)],
            dst_ref=rows.at[span(side * experts + expert)],
            send_sem=go_send.at[index],
            recv_sem=go_recv.at[side, expert],
            device_id=(partner if side else patch, index),
            device_id_type=MESH,
        )

    def back(side, index, part):
        return pltpu.make_async_remote_copy(
            src_ref=produced.at[part, span(side * experts + index)],
            dst_ref=returned.at[part, span(expert)],
            send_sem=back_send.at[part, side, index],
            recv_sem=back_recv.at[part, expert],
            device_id=(partner if side else patch, index),
            device_id_type=MESH,
        )

    def await_rows(side, source):
        pltpu.make_async_copy(
            outgoing.at[span(source)],
            rows.at[span(side * experts + source)],
            go_recv.at[side, source],
        ).wait()

    def await_back(source, part):
        pltpu.make_async_copy(
            produced.at[part, span(source)],
            returned.at[part, span(source)],
            back_recv.at[part, source],
        ).wait()

    @pl.when(end_plane)
    def _():
        for step in range(experts):
            go(1, (expert + step) % experts).start()

    @pl.when(middle_plane)
    def _():
        for step in range(1, experts):
            go(0, (expert + step) % experts).start()
        rows[span(expert), :] = outgoing[span(expert), :]
        for which in chunks[1:]:
            arrived(which, partner)
            transfer(which, TO_MIDDLE, partner).start()
            if which + 1 in chunks:
                transfer(which + 1, TO_MIDDLE, patch, True).start()
        for index in (across, far):
            arrived(1, index)
            transfer(1, TO_CORE, index).start()
        for which in chunks:
            transfer(which, TO_CORE, patch, True).start()
            transfer(which, TO_CORE, partner).start()
        for load in own_loads:
            load.wait()
        for step in range(1, experts):
            await_rows(0, (expert + step) % experts)
        for step in range(experts):
            await_rows(1, (expert + step) % experts)
        for plane in range(4):
            arrived(1, plane * 2 + 1 - core)

        def first_layer(step, carry):
            columns = pl.ds(pl.multiple_of(step * 256, 256), 256)
            hidden[:, columns] = jax.nn.gelu(
                jnp.dot(rows[...], win[:, columns], preferred_element_type=jnp.float32),
                approximate=True,
            ).astype(jnp.bfloat16)
            return carry

        lax.fori_loop(0, ffw // 256, first_layer, 0)

        count = experts * capacity
        for part in range(CHUNKS):
            which = part + 2
            for index in (across, far):
                arrived(which, index)
                transfer(which, TO_CORE, index).start()
            for plane in range(4):
                arrived(which, plane * 2 + 1 - core)
            half = count // 2
            for begin, size in ((count, half), (count + half, half), (0, count)):
                block = slice(begin, begin + size)
                produced[part, block, :] = jnp.dot(
                    hidden[block, :], wout[part], preferred_element_type=jnp.float32
                ).astype(jnp.bfloat16)
                if begin:
                    first = (begin - count) // capacity
                    for index in range(first, first + experts // 2):
                        back(1, index, part).start()
                else:
                    for step in range(1, experts):
                        back(0, (expert + step) % experts, part).start()
            returned[part, span(expert), :] = produced[part, span(expert), :]

    entry = lax.broadcasted_iota(jnp.int32, (tokens, capacity), 1).astype(jnp.float32)
    gates = jax.nn.sigmoid(logits)
    picks = [
        (entry == place[:, index : index + 1]).astype(jnp.float32).astype(jnp.bfloat16)
        for index in range(experts)
    ]
    for part in range(CHUNKS):
        for step in range(1, experts):
            await_back((expert + step) % experts, part)

        @pl.when(end_plane)
        def _():
            await_back(expert, part)

        columns = slice(part * chunk, (part + 1) * chunk)
        mixture = jnp.zeros((tokens, chunk), jnp.float32)
        for index in range(experts):
            picked = jnp.dot(
                picks[index],
                returned[part, index * capacity : (index + 1) * capacity, :],
                preferred_element_type=jnp.float32,
            )
            mixture = mixture + picked * gates[:, index : index + 1]
        out_ref[:, columns] = (
            out_ref[:, columns].astype(jnp.float32) + row_of(5)[:, columns] * mixture
        ).astype(jnp.bfloat16)

    transfer(0, TO_CORE, patch, True).wait_send()
    for index in (partner, across, far):
        transfer(0, TO_CORE, index).wait_send()

    @pl.when(end_plane)
    def _():
        for which in range(1, 2 + CHUNKS):
            transfer(which, TO_PARTNER, patch, True).wait_send()
        for step in range(experts):
            go(1, (expert + step) % experts).wait_send()

    @pl.when(middle_plane)
    def _():
        transfer(0, TO_PARTNER, patch, True).wait_send()
        transfer(0, TO_MIDDLE, patch, True).wait_send()
        transfer(0, TO_MIDDLE, partner).wait_send()
        transfer(0, TO_PARTNER, across).wait_send()
        transfer(0, TO_PARTNER, far).wait_send()
        for which in range(1, 2 + CHUNKS):
            transfer(which, TO_MIDDLE, patch, True).wait_send()
            transfer(which, TO_MIDDLE, partner).wait_send()
            transfer(which, TO_CORE, patch, True).wait_send()
            for index in (partner, across, far):
                transfer(which, TO_CORE, index).wait_send()
        for step in range(1, experts):
            go(0, (expert + step) % experts).wait_send()
        for part in range(CHUNKS):
            for side in (1, 0):
                for step in range(1 - side, experts):
                    back(side, (expert + step) % experts, part).wait_send()


def store_kernel(state_ref, current_ref, out_ref, fresh_ref):
    out_ref[...] = state_ref[...]
    fresh_ref[...] = current_ref[...]


def on_line(latent, stale_kv, modulation, routes, w_qkv, w_attn_out, router, w_in, w_out):
    tokens, width = latent.shape[1:]
    attn = w_attn_out.shape[0]
    experts, patches = lax.axis_size("expert"), lax.axis_size("patch")
    capacity = min(tokens, 5 * tokens // (2 * experts))
    ffw = w_in.shape[2]
    padded = -(-attn // 128) * 128
    slots = experts * capacity
    vmem, hbm = pl.BlockSpec(memory_space=pltpu.VMEM), pl.BlockSpec(memory_space=pl.ANY)
    narrow = jnp.bfloat16
    state, current = pl.pallas_call(
        functools.partial(block_kernel, capacity),
        out_shape=(
            jax.ShapeDtypeStruct((tokens, width), narrow),
            jax.ShapeDtypeStruct((tokens, 2 * attn), narrow),
        ),
        in_specs=[vmem, hbm, vmem, vmem, hbm, hbm, vmem, hbm, hbm],
        out_specs=(vmem, vmem),
        scratch_shapes=[
            pltpu.VMEM((patches * tokens, 2 * attn), narrow),
            pltpu.VMEM(w_qkv.shape[::-1], narrow),
            pltpu.VMEM((padded, width), narrow),
            pltpu.VMEM((width, ffw), narrow),
            pltpu.VMEM((CHUNKS, ffw, width // CHUNKS), narrow),
            pltpu.VMEM((slots, width), narrow),
            pltpu.VMEM((2 * slots, width), narrow),
            pltpu.VMEM((2 * slots, ffw), narrow),
            pltpu.VMEM((CHUNKS, 2 * slots, width // CHUNKS), narrow),
            pltpu.VMEM((CHUNKS, slots, width // CHUNKS), narrow),
            pltpu.VMEM((tokens, padded), jnp.float32),
            pltpu.SemaphoreType.DMA((3 + CHUNKS,)),
            pltpu.SemaphoreType.DMA((2 + CHUNKS, 3, patches)),
            pltpu.SemaphoreType.DMA((2 + CHUNKS, patches)),
            pltpu.SemaphoreType.DMA((experts,)),
            pltpu.SemaphoreType.DMA((2, experts)),
            pltpu.SemaphoreType.DMA((CHUNKS, 2, experts)),
            pltpu.SemaphoreType.DMA((CHUNKS, experts)),
        ],
        compiler_params=pltpu.CompilerParams(
            collective_id=0, has_side_effects=True, vmem_limit_bytes=56 * 1024 * 1024
        ),
    )(
        latent[0], stale_kv[0], jnp.transpose(modulation, (1, 0, 2)), routes[0, 0].T, w_qkv.T,
        w_attn_out, router.T, w_in[0], w_out[0],
    )
    state, current = pl.pallas_call(
        store_kernel,
        out_shape=(
            jax.ShapeDtypeStruct(state.shape, narrow),
            jax.ShapeDtypeStruct(current.shape, narrow),
        ),
        in_specs=[vmem, vmem],
        out_specs=(vmem, vmem),
    )(state, current)
    return (state[None], current[None])


def solution(mesh):
    line_of_four = mesh.shape["patch"] == 8 and mesh.shape["expert"] == 4
    in_specs = (
        P("expert", "patch", None),
        P("expert", "patch", None),
        P(),
        P(None, "expert", "patch", None),
        P(),
        P(),
        P(),
        P("expert", "patch", None),
        P("expert", "patch", None),
    )
    out_specs = (P("expert", "patch", None), P("expert", "patch", None))
    return jax.shard_map(
        on_line if line_of_four else on_device, mesh=mesh, in_specs=in_specs, out_specs=out_specs, check_vma=False
    )
```
